512 devices in a mesh: gx: 32 (over z, y_hi), gy: 16 (over y_lo, x, core).
Axes of the slice: x: 4, y: 4 (y_hi: 2, y_lo: 2; y = y_hi * 2 + y_lo), z: 16, core: 2. Of those that a mesh axis runs over, the one named last changes fastest.
Arguments:
- velocity: float32 [2, 20, 256, 2048], P(None, None, 'gx', 'gy'), may hold values from -6 to 6
- drive: float32 [2, 256, 2048], P(None, 'gx', 'gy'), may hold values from -0.6 to 0.6
- stiffness: float32 [256, 2048], P('gx', 'gy'), may hold values from 0.5 to 2
- thickness: float32 [256, 2048], P('gx', 'gy'), may hold values from 0.5 to 2
- ice_mask: int32 [256, 2048], P('gx', 'gy'), may hold values from 0 to 1
- friction_class: int32 [256, 2048], P('gx', 'gy'), may hold values from 0 to 7
- friction_table: float32 [8], replicated, may hold values from 0.1 to 10
Outputs:
- velocity_out: float32 [2, 20, 256, 2048], P(None, None, 'gx', 'gy')
- residual: float32 [2, 20, 256, 2048], P(None, None, 'gx', 'gy')
The draws below stay inside these ranges and needn't reach their ends.
All inputs are finite; a program needn't handle non-finite values.
Results may differ from the reference program's by a relative error of at most 0.0003.
Values sent between devices are 32-bit elements; how exact they have to be, the bound alone decides.
No kernel may reach another device: no remote copies, remote signals or barrier semaphores. Data moves between devices by JAX's collectives and lax.ppermute only.
A program may use at most 128 MiB of HBM per device.

```python
import math
import jax
import jax.numpy as jnp
from jax import lax

L = 20
CX = 8
PRE = 2
POST = 2
COARSE = 4
NCLASS = 8
NX = 256
NY = 2048


def draw_ice_mask(key, part):
    key = jax.random.fold_in(key, 11)
    rolled = jax.random.randint(key, (NX, NY), 0, 100)
    band_index = jnp.arange(NX, dtype=jnp.int32) // CX % 4
    ice_limit = 30 + 20 * band_index
    return (rolled < ice_limit[:, None]).astype(jnp.int32)


def with_ends(values, stream_key, low, high):
    longest = values.shape.index(max(values.shape))
    spots = []
    for shift in (0, 1):
        where = [jax.random.randint(jax.random.fold_in(stream_key, axis), (), 0, length) for axis, length in enumerate(values.shape)]
        where[longest] = (where[longest] + shift) % values.shape[longest]
        spots.append(tuple(where))
    return values.at[spots[0]].set(low).at[spots[1]].set(high)


def block_scale(key, dims, split, least, largest):
    loudness, own = 1.0, jax.random.fold_in(key, 6)
    for dim, parts in split:
        draws = jnp.exp(jax.random.uniform(jax.random.fold_in(own, dim), (parts,), jnp.float32, least / len(split), largest / len(split)))
        loudness = loudness * jnp.repeat(draws, dims[dim] // parts).reshape([-1 if axis == dim else 1 for axis in range(len(dims))])
    return loudness


def noise(own_key, dims, scale, most, shards=(), kind=jnp.bfloat16):
    values = jax.random.normal(own_key, dims, jnp.float32) * scale
    if len(shards) > 0:
        values = block_scale(own_key, dims, shards, -0.22, 0.18) * values
    return jnp.clip(values, min=-most, max=most).astype(kind)


def setup_inputs(seed: int = 0) -> dict:
    key_of = jax.random.split(jax.random.key(seed), 8)
    velocity = noise(key_of[0], (2, L, NX, NY), 1.0, 6.0, ((2, 32), (3, 16)), jnp.float32)
    drive = noise(key_of[1], (2, NX, NY), 0.1, 0.6, ((1, 32), (2, 16)), jnp.float32)
    stiffness = jnp.clip(jnp.exp(math.log(2.0) - 1.3862944 * jax.random.uniform(key_of[2], (NX, NY), jnp.float32) ** block_scale(key_of[2], (NX, NY), ((0, 32), (1, 16)), -0.2, 0.2)), 0.5, 2.0)
    thickness = jnp.clip(jnp.exp(math.log(2.0) - 1.3862944 * jax.random.uniform(key_of[3], (NX, NY), jnp.float32) ** block_scale(key_of[3], (NX, NY), ((0, 32), (1, 16)), -0.2, 0.2)), 0.5, 2.0)
    ice_mask = draw_ice_mask(jax.random.fold_in(key_of[7], 71), 0)
    friction_class = with_ends(jax.random.randint(key_of[5], (NX, NY), 0, NCLASS), jax.random.fold_in(key_of[5], 1), 0, NCLASS - 1).astype(jnp.int32)
    friction_table = jnp.clip(jnp.exp(jax.random.uniform(key_of[6], (NCLASS,), jnp.float32, math.log(0.1), math.log(10.0))), 0.1, 10.0)
    return {"velocity": velocity, "drive": drive, "stiffness": stiffness, "thickness": thickness, "ice_mask": ice_mask, "friction_class": friction_class, "friction_table": friction_table}


OMEGA = 0.8
EPS0 = 0.01
FACTOR_X = (4.0, 1.0)
FACTOR_Y = (1.0, 4.0)

def viscosity(padded, stiffness, thickness):
    layers = padded.shape[1]
    spacing = thickness / layers
    centre = padded[:, :, 1:-1, 1:-1]
    slope_first = (padded[:, :, 2:, 1:-1] - padded[:, :, :-2, 1:-1]) * 0.5
    slope_second = (padded[:, :, 1:-1, 2:] - padded[:, :, 1:-1, :-2]) * 0.5
    upper_cells = jnp.concatenate([centre[:, 1:], centre[:, -1:]], axis=1)
    lower_cells = jnp.concatenate([centre[:, :1], centre[:, :-1]], axis=1)
    slope_vert = (upper_cells - lower_cells) / (2.0 * spacing)
    shear_sum = slope_second[0] + slope_first[1]
    strain_rate = slope_first[0] * slope_first[0] + slope_second[1] * slope_second[1] + slope_first[0] * slope_second[1] + 0.25 * shear_sum * shear_sum + 0.25 * (slope_vert[0] * slope_vert[0] + slope_vert[1] * slope_vert[1]) + EPS0
    return 0.5 * stiffness * strain_rate ** (-1.0 / 3.0)

def build_operator(padded_eta, ice_float, bed_drag, thickness, scale):
    centre = padded_eta[:, 1:-1, 1:-1]
    east_face = scale * jnp.sqrt(centre * padded_eta[:, 2:, 1:-1])
    west_face = scale * jnp.sqrt(centre * padded_eta[:, :-2, 1:-1])
    north_face = scale * jnp.sqrt(centre * padded_eta[:, 1:-1, 2:])
    south_face = scale * jnp.sqrt(centre * padded_eta[:, 1:-1, :-2])
    layers = centre.shape[0]
    spacing = thickness / layers
    vert_faces = 0.5 * (centre[1:] + centre[:-1]) / (spacing * spacing)
    zero_row = jnp.zeros_like(centre[:1])
    upper_face = jnp.concatenate([vert_faces, zero_row], axis=0)
    lower_face = jnp.concatenate([zero_row, vert_faces], axis=0)
    bed_row = jnp.concatenate([(bed_drag / spacing)[None], jnp.zeros_like(centre[1:])], axis=0)
    common = upper_face + lower_face + bed_row + (1.0 - ice_float)
    diagonal = jnp.stack([FACTOR_X[component] * (east_face + west_face) + FACTOR_Y[component] * (north_face + south_face) + common for component in range(2)])
    return (east_face, west_face, north_face, south_face, upper_face, lower_face, diagonal)

def apply_operator(coeffs, padded):
    east_face, west_face, north_face, south_face, upper_face, lower_face, diagonal = coeffs
    centre = padded[:, :, 1:-1, 1:-1]
    zero_row = jnp.zeros_like(centre[:, :1])
    upper_cells = jnp.concatenate([centre[:, 1:], zero_row], axis=1)
    lower_cells = jnp.concatenate([zero_row, centre[:, :-1]], axis=1)
    result = []
    for component in range(2):
        across = east_face * padded[component, :, 2:, 1:-1] + west_face * padded[component, :, :-2, 1:-1]
        sideways = north_face * padded[component, :, 1:-1, 2:] + south_face * padded[component, :, 1:-1, :-2]
        vertical = upper_face * upper_cells[component] + lower_face * lower_cells[component]
        result.append(diagonal[component] * centre[component] - FACTOR_X[component] * across - FACTOR_Y[component] * sideways - vertical)
    return jnp.stack(result)

def column_solve(coeffs, forcing):
    upper_face, lower_face, diagonal = (coeffs[4], coeffs[5], coeffs[6])
    layers = forcing.shape[1]
    ratios = []
    partials = []
    for layer in range(layers):
        if layer == 0:
            pivot_value = diagonal[:, 0]
            partial_value = forcing[:, 0] / pivot_value
        else:
            pivot_value = diagonal[:, layer] - lower_face[layer] * ratios[-1]
            partial_value = (forcing[:, layer] + lower_face[layer] * partials[-1]) / pivot_value
        ratios.append(upper_face[layer] / pivot_value)
        partials.append(partial_value)
    solved = [partials[-1]]
    for layer in range(layers - 2, -1, -1):
        solved.append(partials[layer] + ratios[layer] * solved[-1])
    return jnp.stack(solved[::-1], axis=1)

def smooth_sweep(coeffs, forcing, field, extend):
    remainder = forcing - apply_operator(coeffs, extend(field))
    return field + OMEGA * column_solve(coeffs, remainder)

def drag_lookup(friction_class, friction_table):
    classes = jnp.arange(friction_table.shape[0], dtype=jnp.int32)
    matches = (friction_class[None] == classes[:, None, None]).astype(jnp.float32)
    return lax.optimization_barrier(jnp.sum(matches * friction_table[:, None, None], axis=0))

def block_mean(field):
    sizes_in = field.shape
    grouped = field.reshape(sizes_in[:-2] + (sizes_in[-2] // 2, 2, sizes_in[-1] // 2, 2))
    return lax.optimization_barrier(jnp.sum(grouped, axis=(-3, -1))) * 0.25

def block_any(field):
    sizes_in = field.shape
    grouped = field.reshape(sizes_in[:-2] + (sizes_in[-2] // 2, 2, sizes_in[-1] // 2, 2))
    return lax.optimization_barrier(jnp.max(grouped, axis=(-3, -1)))

def prolongate(field):
    return jnp.repeat(jnp.repeat(field, 2, axis=-2), 2, axis=-1)

def pad_border(field):
    widths = [(0, 0)] * (field.ndim - 2) + [(1, 1), (1, 1)]
    return jnp.pad(field, widths)

def reference(velocity, drive, stiffness, thickness, ice_mask, friction_class, friction_table):
    ice_float = ice_mask.astype(jnp.float32)
    initial = velocity * ice_float
    viscous = viscosity(pad_border(initial), stiffness, thickness)
    masked = viscous * ice_float
    bed_drag = ice_float * drag_lookup(friction_class, friction_table)
    coeffs = build_operator(pad_border(masked), ice_float, bed_drag, thickness, 1.0)
    forcing = jnp.broadcast_to((drive * ice_float)[:, None], velocity.shape)
    current = initial
    for turn_index in range(PRE):
        current = smooth_sweep(coeffs, forcing, current, pad_border)
    remainder = forcing - apply_operator(coeffs, pad_border(current))
    coarse_mask = block_any(ice_mask).astype(jnp.float32)
    coarse_coeffs = build_operator(pad_border(block_mean(masked)), coarse_mask, block_mean(bed_drag), block_mean(thickness), 0.25)
    coarse_forcing = block_mean(remainder)
    correction = jnp.zeros_like(coarse_forcing)
    for turn_index in range(COARSE):
        correction = smooth_sweep(coarse_coeffs, coarse_forcing, correction, pad_border)
    current = current + ice_float * prolongate(correction)
    for turn_index in range(POST):
        current = smooth_sweep(coeffs, forcing, current, pad_border)
    residual = forcing - apply_operator(coeffs, pad_border(current))
    return (current, residual)
```

```python
import jax
import jax.numpy as jnp
from jax import lax
from jax.experimental import pallas as pl
from jax.experimental.pallas import tpu as pltpu
from jax.sharding import PartitionSpec as P

L = 20
PLANES = 45
STRIPS = 12
F32 = jnp.float32


def iotas(shape=(8, 128)):
    return lax.broadcasted_iota(jnp.int32, shape, 0), lax.broadcasted_iota(jnp.int32, shape, 1)


def pack_kernel(vel, drive, stiff, thick, ice, cls, table, main, strips):
    sub, lane = iotas()
    m = ice[...].astype(F32)
    drag = jnp.zeros((8, 128), F32)
    for i in range(8):
        drag = jnp.where(cls[...] == i, table[i], drag)

    def plane(p):
        if p < 40:
            return vel[p // L, p % L] * m
        return (drive[0] * m, drive[1] * m, 0.5 * stiff[...] * m, thick[...], drag * m)[p - 40]

    for j in range(STRIPS):
        packed = jnp.zeros((8, 128), F32)
        for g in range(4):
            p = 4 * j + g
            if p < PLANES:
                tile = pltpu.roll(plane(p), 4, 0)
                main[p] = tile
                moved = pltpu.roll(tile, (32 * g + 16) % 128, 1)
                packed = jnp.where((lane >= 32 * g) & (lane < 32 * g + 32), moved, packed)
        strips[j] = packed


def neighbours(tiles, sub, lane):
    n = len(tiles[0])
    rows, cols = [], []
    for lt in range(len(tiles)):
        r, c = [], []
        for k in range(n):
            here = tiles[lt][k]
            up = pltpu.roll(jnp.where(sub == 7, tiles[lt][(k - 1) % n], here), 1, 0)
            dn = pltpu.roll(jnp.where(sub == 0, tiles[lt][(k + 1) % n], here), 7, 0)
            r.append((up, dn))
            if len(tiles) == 2:
                other = tiles[1 - lt][k]
                lf = pltpu.roll(jnp.where(lane == 127, other, here), 1, 1)
                rt = pltpu.roll(jnp.where(lane == 0, other, here), 127, 1)
            else:
                lf = pltpu.roll(here, 1, 1)
                rt = pltpu.roll(here, 127, 1)
            c.append((lf, rt))
        rows.append(r)
        cols.append(c)
    return rows, cols


def weighted(component, row_pair, col_pair):
    a = row_pair[0] + row_pair[1]
    b = col_pair[0] + col_pair[1]
    return 4.0 * a + b if component == 0 else a + 4.0 * b


def main_kernel(
    gm2, gm1, g0, gp1, gp2, restrict, expand, vel_out, res_out,
    V, F, Q, E, W, D, C, I, T, X, CA, CB, CE, CF, CX, CQ, CW, CC, CI, CT, PC,
):
    sub, lane = iotas()
    low = sub < 4
    G = [gm2, gm1, g0, gp1, gp2]
    inner = (lane < 16) | (lane >= 112)

    for p in range(PLANES):
        for k in range(5):
            a, b = G[k], G[(k + 1) % 5]
            main = jnp.where(low, a[p], b[p])
            j, g = PLANES + p // 4, p % 4
            rim = jnp.where(low, a[j], b[j])
            rim = pltpu.roll(rim, 128 - (32 * g + 16), 1)
            rim = jnp.where(inner, rim, 0.0)
            for lt, tile in ((0, main), (1, rim)):
                if p < 40:
                    V[p, lt, 8 * k : 8 * k + 8, :] = tile
                else:
                    if p == 43:
                        tile = jnp.where(tile > 0.0, tile, 1.0)
                    F[p - 40, lt, 8 * k : 8 * k + 8, :] = tile

    def rows(k):
        return slice(8 * k, 8 * k + 8)

    root = [[jnp.sqrt(F[2, lt, rows(k), :]) for k in range(5)] for lt in range(2)]
    quarter = [[25.0 / (F[3, lt, rows(k), :] * F[3, lt, rows(k), :]) for k in range(5)] for lt in range(2)]
    for lt in range(2):
        for k in range(5):
            T[0, lt, rows(k), :] = root[lt][k]
            T[1, lt, rows(k), :] = quarter[lt][k]

    def visc(z, _):
        after, before = jnp.minimum(z + 1, L - 1), jnp.maximum(z - 1, 0)
        u = [[V[z, lt, rows(k), :] for k in range(5)] for lt in range(2)]
        ur, uc = neighbours(u, sub, lane)
        ux = [[ur[lt][k][1] - ur[lt][k][0] for k in range(5)] for lt in range(2)]
        uy = [[uc[lt][k][1] - uc[lt][k][0] for k in range(5)] for lt in range(2)]
        v = [[V[z + L, lt, rows(k), :] for k in range(5)] for lt in range(2)]
        vr, vc = neighbours(v, sub, lane)
        for lt in range(2):
            for k in range(5):
                vx = vr[lt][k][1] - vr[lt][k][0]
                vy = vc[lt][k][1] - vc[lt][k][0]
                uz = V[after, lt, rows(k), :] - V[before, lt, rows(k), :]
                vz = V[after + L, lt, rows(k), :] - V[before + L, lt, rows(k), :]
                x, y = ux[lt][k], uy[lt][k]
                shear = y + vx
                plane = x * x + vy * vy + x * vy + 0.25 * (shear * shear)
                eps = 0.25 * plane + T[1, lt, rows(k), :] * (uz * uz + vz * vz) + 0.01
                q = T[0, lt, rows(k), :] * jnp.exp(jnp.log(eps) * (-1.0 / 6.0))
                Q[z, lt, rows(k), :] = q
                if k < 4:
                    E[z, lt, rows(k), :] = q * q
        return 0

    lax.fori_loop(0, L, visc, 0)

    def factor(z, carry):
        top = jnp.where(z < L - 1, 1.0, 0.0)
        bed = jnp.where(z == 0, 1.0, 0.0)
        after = jnp.minimum(z + 1, L - 1)
        q = [[Q[z, lt, rows(k), :] for k in range(5)] for lt in range(2)]
        qr, qc = neighbours(q, sub, lane)
        out = []
        for lt in range(2):
            for k in range(4):
                i = lt * 4 + k
                wbefore, cx, cy = carry[3 * i : 3 * i + 3]
                h = F[3, lt, rows(k), :]
                ih = 20.0 / h
                w = (E[z, lt, rows(k), :] + E[after, lt, rows(k), :]) * (0.5 * top * (ih * ih))
                off = jnp.where(F[2, lt, rows(k), :] > 0.0, 0.0, 1.0)
                common = w + wbefore + bed * (F[4, lt, rows(k), :] * ih) + off
                W[z, lt, rows(k), :] = w
                new = [w]
                for component, cb in ((0, cx), (1, cy)):
                    d = q[lt][k] * weighted(component, qr[lt][k], qc[lt][k]) + common
                    inv = 1.0 / (d - wbefore * cb)
                    c = w * inv
                    D[component * L + z, lt, rows(k), :] = d
                    I[component * L + z, lt, rows(k), :] = inv
                    C[component * L + z, lt, rows(k), :] = c
                    new.append(c)
                out += new
        return tuple(out)

    zero = jnp.zeros((8, 128), F32)
    lax.fori_loop(0, L, factor, (zero,) * 24)

    def forward(src, tiles, rim_tile):
        n = len(tiles)
        use = tiles + ([rim_tile] if rim_tile is not None else [])

        def step(z, carry):
            out = []
            for component in range(2):
                p = component * L + z
                q = [[Q[z, lt, rows(k), :] for k in use] for lt in range(2)]
                y = [[q[lt][i] * src[p, lt, rows(k), :] for i, k in enumerate(use)] for lt in range(2)]
                yr, yc = neighbours(y, sub, lane)
                for lt in range(2):
                    for i, k in enumerate(tiles):
                        t = F[component, lt, rows(k), :] + q[lt][i] * weighted(component, yr[lt][i], yc[lt][i])
                        t = t + carry[(component * 2 + lt) * n + i]
                        T[p, lt, rows(k), :] = t
                        out.append(C[p, lt, rows(k), :] * t)
            return tuple(out)

        lax.fori_loop(0, L, step, (zero,) * (4 * n))

    def backward(src, dst, tiles):
        n = len(tiles)

        def step(s, carry):
            z = L - 1 - s
            out = []
            for component in range(2):
                p = component * L + z
                for lt in range(2):
                    for i, k in enumerate(tiles):
                        new = I[p, lt, rows(k), :] * T[p, lt, rows(k), :] + C[p, lt, rows(k), :] * carry[(component * 2 + lt) * n + i]
                        dst[p, lt, rows(k), :] = 0.2 * src[p, lt, rows(k), :] + 0.8 * new
                        out.append(new)
            return tuple(out)

        lax.fori_loop(0, L, step, (zero,) * (4 * n))

    def remainder(src, tiles, put):
        n = len(tiles)

        def step(z, carry):
            after = jnp.minimum(z + 1, L - 1)
            out = []
            for component in range(2):
                p = component * L + z
                x = [[src[p, lt, rows(k), :] for k in tiles] for lt in range(2)]
                q = [[Q[z, lt, rows(k), :] for k in tiles] for lt in range(2)]
                y = [[q[lt][i] * x[lt][i] for i in range(n)] for lt in range(2)]
                yr, yc = neighbours(y, sub, lane)
                got = []
                for lt in range(2):
                    for i, k in enumerate(tiles):
                        w = W[z, lt, rows(k), :]
                        r = F[component, lt, rows(k), :] + q[lt][i] * weighted(component, yr[lt][i], yc[lt][i])
                        r = r - D[p, lt, rows(k), :] * x[lt][i]
                        r = r + w * src[after + component * L, lt, rows(k), :] + carry[(component * 2 + lt) * n + i]
                        got.append(r)
                        out.append(w * x[lt][i])
                put(component, z, got)
            return tuple(out)

        lax.fori_loop(0, L, step, (zero,) * (4 * n))

    pre = [0, 1, 2, 3]
    forward(V, pre, 4)
    backward(V, X, pre)
    forward(X, pre, None)
    backward(X, X, pre)

    def put_rem(component, z, got):
        for lt in range(2):
            for i, k in enumerate(pre):
                T[component * L + z, lt, rows(k), :] = got[lt * 4 + i]

    remainder(X, pre, put_rem)

    even, odd = pl.ds(0, 16, stride=2), pl.ds(1, 16, stride=2)

    def gather(p, _):
        for lt in range(2):
            CA[lt, pl.ds(pl.multiple_of(p * 16, 16), 16), :] = T[p, lt, even, :] + T[p, lt, odd, :]
        return 0

    lax.fori_loop(0, 40, gather, 0)

    def gather_eta(z, _):
        for lt in range(2):
            CA[lt, pl.ds(pl.multiple_of((z + 40) * 16, 16), 16), :] = E[z, lt, even, :] + E[z, lt, odd, :]
        return 0

    lax.fori_loop(0, L, gather_eta, 0)
    for i in range(3):
        for lt in range(2):
            CA[lt, (60 + i) * 16 : (61 + i) * 16, :] = F[2 + i, lt, even, :] + F[2 + i, lt, odd, :]
    CB[...] = jnp.dot(
        CA[0], restrict[0], precision=lax.Precision.HIGHEST, preferred_element_type=F32
    ) + jnp.dot(CA[1], restrict[1], precision=lax.Precision.HIGHEST, preferred_element_type=F32)

    cmask = [jnp.where(CB[960 + 8 * k : 968 + 8 * k, :] > 0.0, 0.0, 1.0) for k in range(2)]
    cthick = [CB[976 + 8 * k : 984 + 8 * k, :] for k in range(2)]
    cih = [20.0 / jnp.where(t > 0.0, t, 1.0) for t in cthick]
    cdrag = [CB[992 + 8 * k : 1000 + 8 * k, :] * cih[k] for k in range(2)]

    def at(p, k):
        return pl.ds(pl.multiple_of(p * 16 + 8 * k, 8), 8)

    def coarse_factor(z, carry):
        top = jnp.where(z < L - 1, 1.0, 0.0)
        bed = jnp.where(z == 0, 1.0, 0.0)
        after = jnp.minimum(z + 1, L - 1)
        e = [CB[at(40 + z, k), :] for k in range(2)]
        q = [[0.5 * jnp.sqrt(e[k]) for k in range(2)]]
        qr, qc = neighbours(q, sub, lane)
        out = []
        for k in range(2):
            wbefore, cx, cy = carry[3 * k : 3 * k + 3]
            w = (e[k] + CB[at(40 + after, k), :]) * (0.5 * top * (cih[k] * cih[k]))
            common = w + wbefore + bed * cdrag[k] + cmask[k]
            CQ[at(z, k), :] = q[0][k]
            new = [w]
            for component, cb in ((0, cx), (1, cy)):
                d = q[0][k] * weighted(component, qr[0][k], qc[0][k]) + common
                inv = 1.0 / (d - wbefore * cb)
                c = w * inv
                CI[at(component * L + z, k), :] = inv
                CC[at(component * L + z, k), :] = c
                new.append(c)
            out += new
        return tuple(out)

    lax.fori_loop(0, L, coarse_factor, (zero,) * 6)

    for turn in range(4):

        def coarse_forward(z, carry, turn=turn):
            out = []
            for component in range(2):
                p = component * L + z
                if turn > 0:
                    q = [CQ[at(z, k), :] for k in range(2)]
                    y = [[q[k] * CX[at(p, k), :] for k in range(2)]]
                    yr, yc = neighbours(y, sub, lane)
                for k in range(2):
                    t = CB[at(p, k), :] + carry[component * 2 + k]
                    if turn > 0:
                        t = t + q[k] * weighted(component, yr[0][k], yc[0][k])
                    CT[at(p, k), :] = t
                    out.append(CC[at(p, k), :] * t)
            return tuple(out)

        lax.fori_loop(0, L, coarse_forward, (zero,) * 4)

        def coarse_backward(s, carry, turn=turn):
            z = L - 1 - s
            out = []
            for component in range(2):
                p = component * L + z
                for k in range(2):
                    new = CI[at(p, k), :] * CT[at(p, k), :] + CC[at(p, k), :] * carry[component * 2 + k]
                    if turn > 0:
                        CX[at(p, k), :] = 0.2 * CX[at(p, k), :] + 0.8 * new
                    else:
                        CX[at(p, k), :] = 0.8 * new
                    out.append(new)
            return tuple(out)

        lax.fori_loop(0, L, coarse_backward, (zero,) * 4)

    def spread(p, _):
        CE[pl.ds(pl.multiple_of(p * 8, 8), 8), :] = pltpu.roll(
            jnp.where(low, CX[at(p, 1), :], CX[at(p, 0), :]), 4, 0
        )
        return 0

    lax.fori_loop(0, 40, spread, 0)
    for lt in range(2):
        CF[lt] = jnp.dot(CE[...], expand[lt], precision=lax.Precision.HIGHEST, preferred_element_type=F32)

    def correct(p, _):
        for lt in range(2):
            tile = CF[lt, pl.ds(pl.multiple_of(p * 8, 8), 8), :]
            PC[p, lt, pl.ds(0, 8, stride=2), :] = tile
            PC[p, lt, pl.ds(1, 8, stride=2), :] = tile
            for k in (1, 2):
                m = jnp.where(F[2, lt, rows(k), :] > 0.0, 1.0, 0.0)
                X[p, lt, rows(k), :] = X[p, lt, rows(k), :] + m * PC[p, lt, rows(k - 1), :]
        return 0

    lax.fori_loop(0, 40, correct, 0)

    post = [1, 2]
    for _ in range(2):
        forward(X, post, None)
        backward(X, X, post)

    def put_res(component, z, got):
        res_out[component, z] = pltpu.roll(jnp.where(low, got[1], got[0]), 4, 0)
        p = component * L + z
        vel_out[component, z] = pltpu.roll(jnp.where(low, X[p, 0, rows(2), :], X[p, 0, rows(1), :]), 4, 0)

    remainder(X, post, put_res)


def transfer_matrices():
    lane = jnp.arange(128)
    main = lane // 2
    rim = jnp.where(lane < 16, 64 + lane // 2, jnp.where(lane >= 112, 120 + (lane - 112) // 2, -1))
    hits = jnp.stack([main, rim])[:, :, None] == lane[None, None, :]
    restrict = jnp.where(hits, 0.25, 0.0).astype(F32)
    expand = jnp.where(hits, 1.0, 0.0).astype(F32).transpose(0, 2, 1)
    return restrict, expand


def shift(axis, by):
    count = lax.axis_size(axis)
    return [(i, i + by) for i in range(count) if 0 <= i + by < count]


def per_device(velocity, drive, stiffness, thickness, ice_mask, friction_class, friction_table):
    vmem = pl.BlockSpec(memory_space=pltpu.VMEM)
    smem = pl.BlockSpec(memory_space=pltpu.SMEM)
    main, strips = pl.pallas_call(
        pack_kernel,
        out_shape=(jax.ShapeDtypeStruct((PLANES, 8, 128), F32), jax.ShapeDtypeStruct((STRIPS, 8, 128), F32)),
        in_specs=[vmem] * 6 + [smem],
        out_specs=(vmem, vmem),
        name="pack",
    )(velocity, drive, stiffness, thickness, ice_mask, friction_class, friction_table)
    left = lax.ppermute(strips, "gy", shift("gy", 1))
    right = lax.ppermute(strips, "gy", shift("gy", -1))
    lane = lax.broadcasted_iota(jnp.int32, strips.shape, 2)
    rim = jnp.where(lane % 32 < 16, left, right)
    whole = jnp.concatenate([main, rim], axis=0)
    parts = [whole if by == 0 else lax.ppermute(whole, "gx", shift("gx", -by)) for by in (-2, -1, 0, 1, 2)]
    restrict, expand = transfer_matrices()
    fine = lambda n, r: pltpu.VMEM((n, 2, r, 128), F32)
    coarse = lambda n: pltpu.VMEM((16 * n, 128), F32)
    out = jax.ShapeDtypeStruct((2, L, 8, 128), F32)
    return pl.pallas_call(
        main_kernel,
        out_shape=(out, out),
        in_specs=[vmem] * 7,
        out_specs=(vmem, vmem),
        scratch_shapes=[
            fine(40, 40), fine(5, 40), fine(20, 40), fine(20, 32), fine(20, 32), fine(40, 32), fine(40, 32), fine(40, 32),
            fine(40, 40), fine(40, 32),
            pltpu.VMEM((2, 63 * 16, 128), F32), coarse(63), pltpu.VMEM((320, 128), F32), pltpu.VMEM((2, 320, 128), F32),
            coarse(40), coarse(20), coarse(20), coarse(40), coarse(40), coarse(40), fine(40, 16),
        ],
        compiler_params=pltpu.CompilerParams(vmem_limit_bytes=48 * 1024 * 1024),
        name="cycle",
    )(*parts, restrict, expand)


def solution(mesh):
    return jax.shard_map(
        per_device,
        mesh=mesh,
        in_specs=(
            P(None, None, "gx", "gy"),
            P(None, "gx", "gy"),
            P("gx", "gy"),
            P("gx", "gy"),
            P("gx", "gy"),
            P("gx", "gy"),
            P(),
        ),
        out_specs=(P(None, None, "gx", "gy"), P(None, None, "gx", "gy")),
        check_vma=False,
    )
```

```python
import jax
import jax.numpy as jnp
from jax import lax
from jax.experimental import pallas as pl
from jax.experimental.pallas import tpu as pltpu
from jax.sharding import PartitionSpec as P

L = 20
PLANES = 45
STRIPS = 12
F32 = jnp.float32
UNROLL = 20


def iotas(shape=(8, 128)):
    return lax.broadcasted_iota(jnp.int32, shape, 0), lax.broadcasted_iota(jnp.int32, shape, 1)


def pack_kernel(vel, drive, stiff, thick, ice, cls, table, main, strips):
    sub, lane = iotas()
    m = ice[...].astype(F32)
    drag = jnp.zeros((8, 128), F32)
    for i in range(8):
        drag = jnp.where(cls[...] == i, table[i], drag)

    def plane(p):
        if p < 40:
            return vel[p // L, p % L] * m
        return (drive[0] * m, drive[1] * m, 0.5 * stiff[...] * m, thick[...], drag * m)[p - 40]

    for j in range(STRIPS):
        packed = jnp.zeros((8, 128), F32)
        for g in range(4):
            p = 4 * j + g
            if p < PLANES:
                tile = pltpu.roll(plane(p), 4, 0)
                main[p] = tile
                moved = pltpu.roll(tile, (32 * g + 16) % 128, 1)
                packed = jnp.where((lane >= 32 * g) & (lane < 32 * g + 32), moved, packed)
        strips[j] = packed


def neighbours(tiles, sub, lane):
    n = len(tiles[0])
    rows, cols = [], []
    for lt in range(len(tiles)):
        r, c = [], []
        for k in range(n):
            here = tiles[lt][k]
            up = pltpu.roll(jnp.where(sub == 7, tiles[lt][(k - 1) % n], here), 1, 0)
            dn = pltpu.roll(jnp.where(sub == 0, tiles[lt][(k + 1) % n], here), 7, 0)
            r.append((up, dn))
            if len(tiles) == 2:
                other = tiles[1 - lt][k]
                lf = pltpu.roll(jnp.where(lane == 127, other, here), 1, 1)
                rt = pltpu.roll(jnp.where(lane == 0, other, here), 127, 1)
            else:
                lf = pltpu.roll(here, 1, 1)
                rt = pltpu.roll(here, 127, 1)
            c.append((lf, rt))
        rows.append(r)
        cols.append(c)
    return rows, cols


def weighted(component, row_pair, col_pair):
    a = row_pair[0] + row_pair[1]
    b = col_pair[0] + col_pair[1]
    return 4.0 * a + b if component == 0 else a + 4.0 * b


def main_kernel(
    gm2, gm1, g0, gp1, gp2, restrict, expand, vel_out, res_out,
    V, F, Q, E, W, D, C, I, T, X, CA, CB, CE, CF, CX, CQ, CW, CC, CI, CT, PC,
):
    sub, lane = iotas()
    low = sub < 4
    G = [gm2, gm1, g0, gp1, gp2]
    inner = (lane < 16) | (lane >= 112)

    for p in range(PLANES):
        for k in range(5):
            a, b = G[k], G[(k + 1) % 5]
            main = jnp.where(low, a[p], b[p])
            j, g = PLANES + p // 4, p % 4
            rim = jnp.where(low, a[j], b[j])
            rim = pltpu.roll(rim, 128 - (32 * g + 16), 1)
            rim = jnp.where(inner, rim, 0.0)
            for lt, tile in ((0, main), (1, rim)):
                if p < 40:
                    V[p, lt, 8 * k : 8 * k + 8, :] = tile
                else:
                    if p == 43:
                        tile = jnp.where(tile > 0.0, tile, 1.0)
                    F[p - 40, lt, 8 * k : 8 * k + 8, :] = tile

    def rows(k):
        return slice(8 * k, 8 * k + 8)

    root = [[jnp.sqrt(F[2, lt, rows(k), :]) for k in range(5)] for lt in range(2)]
    quarter = [[25.0 / (F[3, lt, rows(k), :] * F[3, lt, rows(k), :]) for k in range(5)] for lt in range(2)]
    for lt in range(2):
        for k in range(5):
            T[0, lt, rows(k), :] = root[lt][k]
            T[1, lt, rows(k), :] = quarter[lt][k]

    def visc(z, _):
        after, before = jnp.minimum(z + 1, L - 1), jnp.maximum(z - 1, 0)
        u = [[V[z, lt, rows(k), :] for k in range(5)] for lt in range(2)]
        ur, uc = neighbours(u, sub, lane)
        ux = [[ur[lt][k][1] - ur[lt][k][0] for k in range(5)] for lt in range(2)]
        uy = [[uc[lt][k][1] - uc[lt][k][0] for k in range(5)] for lt in range(2)]
        v = [[V[z + L, lt, rows(k), :] for k in range(5)] for lt in range(2)]
        vr, vc = neighbours(v, sub, lane)
        for lt in range(2):
            for k in range(5):
                vx = vr[lt][k][1] - vr[lt][k][0]
                vy = vc[lt][k][1] - vc[lt][k][0]
                uz = V[after, lt, rows(k), :] - V[before, lt, rows(k), :]
                vz = V[after + L, lt, rows(k), :] - V[before + L, lt, rows(k), :]
                x, y = ux[lt][k], uy[lt][k]
                shear = y + vx
                plane = x * x + vy * vy + x * vy + 0.25 * (shear * shear)
                eps = 0.25 * plane + T[1, lt, rows(k), :] * (uz * uz + vz * vz) + 0.01
                q = T[0, lt, rows(k), :] * jnp.exp(jnp.log(eps) * (-1.0 / 6.0))
                Q[z, lt, rows(k), :] = q
                if k < 4:
                    E[z, lt, rows(k), :] = q * q
        return 0

    lax.fori_loop(0, L, visc, 0, unroll=UNROLL)

    def factor(z, carry):
        top = jnp.where(z < L - 1, 1.0, 0.0)
        bed = jnp.where(z == 0, 1.0, 0.0)
        after = jnp.minimum(z + 1, L - 1)
        q = [[Q[z, lt, rows(k), :] for k in range(5)] for lt in range(2)]
        qr, qc = neighbours(q, sub, lane)
        out = []
        for lt in range(2):
            for k in range(4):
                i = lt * 4 + k
                wbefore, cx, cy = carry[3 * i : 3 * i + 3]
                h = F[3, lt, rows(k), :]
                ih = 20.0 / h
                w = (E[z, lt, rows(k), :] + E[after, lt, rows(k), :]) * (0.5 * top * (ih * ih))
                off = jnp.where(F[2, lt, rows(k), :] > 0.0, 0.0, 1.0)
                common = w + wbefore + bed * (F[4, lt, rows(k), :] * ih) + off
                W[z, lt, rows(k), :] = w
                new = [w]
                for component, cb in ((0, cx), (1, cy)):
                    d = q[lt][k] * weighted(component, qr[lt][k], qc[lt][k]) + common
                    inv = 1.0 / (d - wbefore * cb)
                    c = w * inv
                    D[component * L + z, lt, rows(k), :] = d
                    I[component * L + z, lt, rows(k), :] = inv
                    C[component * L + z, lt, rows(k), :] = c
                    new.append(c)
                out += new
        return tuple(out)

    zero = jnp.zeros((8, 128), F32)
    lax.fori_loop(0, L, factor, (zero,) * 24, unroll=UNROLL)

    def forward(src, tiles, rim_tile):
        n = len(tiles)
        use = tiles + ([rim_tile] if rim_tile is not None else [])

        def step(z, carry):
            out = []
            for component in range(2):
                p = component * L + z
                q = [[Q[z, lt, rows(k), :] for k in use] for lt in range(2)]
                y = [[q[lt][i] * src[p, lt, rows(k), :] for i, k in enumerate(use)] for lt in range(2)]
                yr, yc = neighbours(y, sub, lane)
                for lt in range(2):
                    for i, k in enumerate(tiles):
                        t = F[component, lt, rows(k), :] + q[lt][i] * weighted(component, yr[lt][i], yc[lt][i])
                        t = t + carry[(component * 2 + lt) * n + i]
                        T[p, lt, rows(k), :] = t
                        out.append(C[p, lt, rows(k), :] * t)
            return tuple(out)

        lax.fori_loop(0, L, step, (zero,) * (4 * n), unroll=UNROLL)

    def backward(src, dst, tiles):
        n = len(tiles)

        def step(s, carry):
            z = L - 1 - s
            out = []
            for component in range(2):
                p = component * L + z
                for lt in range(2):
                    for i, k in enumerate(tiles):
                        new = I[p, lt, rows(k), :] * T[p, lt, rows(k), :] + C[p, lt, rows(k), :] * carry[(component * 2 + lt) * n + i]
                        dst[p, lt, rows(k), :] = 0.2 * src[p, lt, rows(k), :] + 0.8 * new
                        out.append(new)
            return tuple(out)

        lax.fori_loop(0, L, step, (zero,) * (4 * n), unroll=UNROLL)

    def remainder(src, tiles, put):
        n = len(tiles)

        def step(z, carry):
            after = jnp.minimum(z + 1, L - 1)
            out = []
            for component in range(2):
                p = component * L + z
                x = [[src[p, lt, rows(k), :] for k in tiles] for lt in range(2)]
                q = [[Q[z, lt, rows(k), :] for k in tiles] for lt in range(2)]
                y = [[q[lt][i] * x[lt][i] for i in range(n)] for lt in range(2)]
                yr, yc = neighbours(y, sub, lane)
                got = []
                for lt in range(2):
                    for i, k in enumerate(tiles):
                        w = W[z, lt, rows(k), :]
                        r = F[component, lt, rows(k), :] + q[lt][i] * weighted(component, yr[lt][i], yc[lt][i])
                        r = r - D[p, lt, rows(k), :] * x[lt][i]
                        r = r + w * src[after + component * L, lt, rows(k), :] + carry[(component * 2 + lt) * n + i]
                        got.append(r)
                        out.append(w * x[lt][i])
                put(component, z, got)
            return tuple(out)

        lax.fori_loop(0, L, step, (zero,) * (4 * n), unroll=UNROLL)

    pre = [0, 1, 2, 3]
    forward(V, pre, 4)
    backward(V, X, pre)
    forward(X, pre, None)
    backward(X, X, pre)

    def put_rem(component, z, got):
        for lt in range(2):
            for i, k in enumerate(pre):
                T[component * L + z, lt, rows(k), :] = got[lt * 4 + i]

    remainder(X, pre, put_rem)

    even, odd = pl.ds(0, 16, stride=2), pl.ds(1, 16, stride=2)

    def gather(p, _):
        for lt in range(2):
            CA[lt, pl.ds(pl.multiple_of(p * 16, 16), 16), :] = T[p, lt, even, :] + T[p, lt, odd, :]
        return 0

    lax.fori_loop(0, 40, gather, 0, unroll=UNROLL)

    def gather_eta(z, _):
        for lt in range(2):
            CA[lt, pl.ds(pl.multiple_of((z + 40) * 16, 16), 16), :] = E[z, lt, even, :] + E[z, lt, odd, :]
        return 0

    lax.fori_loop(0, L, gather_eta, 0, unroll=UNROLL)
    for i in range(3):
        for lt in range(2):
            CA[lt, (60 + i) * 16 : (61 + i) * 16, :] = F[2 + i, lt, even, :] + F[2 + i, lt, odd, :]
    CB[...] = jnp.dot(
        CA[0], restrict[0], precision=lax.Precision.HIGHEST, preferred_element_type=F32
    ) + jnp.dot(CA[1], restrict[1], precision=lax.Precision.HIGHEST, preferred_element_type=F32)

    cmask = [jnp.where(CB[960 + 8 * k : 968 + 8 * k, :] > 0.0, 0.0, 1.0) for k in range(2)]
    cthick = [CB[976 + 8 * k : 984 + 8 * k, :] for k in range(2)]
    cih = [20.0 / jnp.where(t > 0.0, t, 1.0) for t in cthick]
    cdrag = [CB[992 + 8 * k : 1000 + 8 * k, :] * cih[k] for k in range(2)]

    def at(p, k):
        return pl.ds(pl.multiple_of(p * 16 + 8 * k, 8), 8)

    def coarse_factor(z, carry):
        top = jnp.where(z < L - 1, 1.0, 0.0)
        bed = jnp.where(z == 0, 1.0, 0.0)
        after = jnp.minimum(z + 1, L - 1)
        e = [CB[at(40 + z, k), :] for k in range(2)]
        q = [[0.5 * jnp.sqrt(e[k]) for k in range(2)]]
        qr, qc = neighbours(q, sub, lane)
        out = []
        for k in range(2):
            wbefore, cx, cy = carry[3 * k : 3 * k + 3]
            w = (e[k] + CB[at(40 + after, k), :]) * (0.5 * top * (cih[k] * cih[k]))
            common = w + wbefore + bed * cdrag[k] + cmask[k]
            CQ[at(z, k), :] = q[0][k]
            new = [w]
            for component, cb in ((0, cx), (1, cy)):
                d = q[0][k] * weighted(component, qr[0][k], qc[0][k]) + common
                inv = 1.0 / (d - wbefore * cb)
                c = w * inv
                CI[at(component * L + z, k), :] = inv
                CC[at(component * L + z, k), :] = c
                new.append(c)
            out += new
        return tuple(out)

    lax.fori_loop(0, L, coarse_factor, (zero,) * 6, unroll=UNROLL)

    for turn in range(4):

        def coarse_forward(z, carry, turn=turn):
            out = []
            for component in range(2):
                p = component * L + z
                if turn > 0:
                    q = [CQ[at(z, k), :] for k in range(2)]
                    y = [[q[k] * CX[at(p, k), :] for k in range(2)]]
                    yr, yc = neighbours(y, sub, lane)
                for k in range(2):
                    t = CB[at(p, k), :] + carry[component * 2 + k]
                    if turn > 0:
                        t = t + q[k] * weighted(component, yr[0][k], yc[0][k])
                    CT[at(p, k), :] = t
                    out.append(CC[at(p, k), :] * t)
            return tuple(out)

        lax.fori_loop(0, L, coarse_forward, (zero,) * 4, unroll=UNROLL)

        def coarse_backward(s, carry, turn=turn):
            z = L - 1 - s
            out = []
            for component in range(2):
                p = component * L + z
                for k in range(2):
                    new = CI[at(p, k), :] * CT[at(p, k), :] + CC[at(p, k), :] * carry[component * 2 + k]
                    if turn > 0:
                        CX[at(p, k), :] = 0.2 * CX[at(p, k), :] + 0.8 * new
                    else:
                        CX[at(p, k), :] = 0.8 * new
                    out.append(new)
            return tuple(out)

        lax.fori_loop(0, L, coarse_backward, (zero,) * 4, unroll=UNROLL)

    def spread(p, _):
        CE[pl.ds(pl.multiple_of(p * 8, 8), 8), :] = pltpu.roll(
            jnp.where(low, CX[at(p, 1), :], CX[at(p, 0), :]), 4, 0
        )
        return 0

    lax.fori_loop(0, 40, spread, 0, unroll=UNROLL)
    for lt in range(2):
        CF[lt] = jnp.dot(CE[...], expand[lt], precision=lax.Precision.HIGHEST, preferred_element_type=F32)

    def correct(p, _):
        for lt in range(2):
            tile = CF[lt, pl.ds(pl.multiple_of(p * 8, 8), 8), :]
            PC[p, lt, pl.ds(0, 8, stride=2), :] = tile
            PC[p, lt, pl.ds(1, 8, stride=2), :] = tile
            for k in (1, 2):
                m = jnp.where(F[2, lt, rows(k), :] > 0.0, 1.0, 0.0)
                X[p, lt, rows(k), :] = X[p, lt, rows(k), :] + m * PC[p, lt, rows(k - 1), :]
        return 0

    lax.fori_loop(0, 40, correct, 0, unroll=UNROLL)

    post = [1, 2]
    for _ in range(2):
        forward(X, post, None)
        backward(X, X, post)

    def put_res(component, z, got):
        res_out[component, z] = pltpu.roll(jnp.where(low, got[1], got[0]), 4, 0)
        p = component * L + z
        vel_out[component, z] = pltpu.roll(jnp.where(low, X[p, 0, rows(2), :], X[p, 0, rows(1), :]), 4, 0)

    remainder(X, post, put_res)


def transfer_matrices():
    lane = jnp.arange(128)
    main = lane // 2
    rim = jnp.where(lane < 16, 64 + lane // 2, jnp.where(lane >= 112, 120 + (lane - 112) // 2, -1))
    hits = jnp.stack([main, rim])[:, :, None] == lane[None, None, :]
    restrict = jnp.where(hits, 0.25, 0.0).astype(F32)
    expand = jnp.where(hits, 1.0, 0.0).astype(F32).transpose(0, 2, 1)
    return restrict, expand


def shift(axis, by):
    count = lax.axis_size(axis)
    return [(i, i + by) for i in range(count) if 0 <= i + by < count]


def per_device(velocity, drive, stiffness, thickness, ice_mask, friction_class, friction_table):
    vmem = pl.BlockSpec(memory_space=pltpu.VMEM)
    smem = pl.BlockSpec(memory_space=pltpu.SMEM)
    main, strips = pl.pallas_call(
        pack_kernel,
        out_shape=(jax.ShapeDtypeStruct((PLANES, 8, 128), F32), jax.ShapeDtypeStruct((STRIPS, 8, 128), F32)),
        in_specs=[vmem] * 6 + [smem],
        out_specs=(vmem, vmem),
        name="pack",
    )(velocity, drive, stiffness, thickness, ice_mask, friction_class, friction_table)
    left = lax.ppermute(strips, "gy", shift("gy", 1))
    right = lax.ppermute(strips, "gy", shift("gy", -1))
    lane = lax.broadcasted_iota(jnp.int32, strips.shape, 2)
    rim = jnp.where(lane % 32 < 16, left, right)
    whole = jnp.concatenate([main, rim], axis=0)
    parts = [whole if by == 0 else lax.ppermute(whole, "gx", shift("gx", -by)) for by in (-2, -1, 0, 1, 2)]
    restrict, expand = transfer_matrices()
    fine = lambda n, r: pltpu.VMEM((n, 2, r, 128), F32)
    coarse = lambda n: pltpu.VMEM((16 * n, 128), F32)
    out = jax.ShapeDtypeStruct((2, L, 8, 128), F32)
    return pl.pallas_call(
        main_kernel,
        out_shape=(out, out),
        in_specs=[vmem] * 7,
        out_specs=(vmem, vmem),
        scratch_shapes=[
            fine(40, 40), fine(5, 40), fine(20, 40), fine(20, 32), fine(20, 32), fine(40, 32), fine(40, 32), fine(40, 32),
            fine(40, 40), fine(40, 32),
            pltpu.VMEM((2, 63 * 16, 128), F32), coarse(63), pltpu.VMEM((320, 128), F32), pltpu.VMEM((2, 320, 128), F32),
            coarse(40), coarse(20), coarse(20), coarse(40), coarse(40), coarse(40), fine(40, 16),
        ],
        compiler_params=pltpu.CompilerParams(vmem_limit_bytes=48 * 1024 * 1024),
        name="cycle",
    )(*parts, restrict, expand)


def solution(mesh):
    return jax.shard_map(
        per_device,
        mesh=mesh,
        in_specs=(
            P(None, None, "gx", "gy"),
            P(None, "gx", "gy"),
            P("gx", "gy"),
            P("gx", "gy"),
            P("gx", "gy"),
            P("gx", "gy"),
            P(),
        ),
        out_specs=(P(None, None, "gx", "gy"), P(None, None, "gx", "gy")),
        check_vma=False,
    )
```

```python
import jax
import jax.numpy as jnp
from jax import lax
from jax.experimental import pallas as pl
from jax.experimental.pallas import tpu as pltpu
from jax.sharding import PartitionSpec as P

L = 20
PLANES = 45
STRIPS = 12
F32 = jnp.float32
UNROLL = 20


def iotas(shape=(8, 128)):
    return lax.broadcasted_iota(jnp.int32, shape, 0), lax.broadcasted_iota(jnp.int32, shape, 1)


def pack_kernel(vel, drive, stiff, thick, ice, cls, table, main, strips):
    sub, lane = iotas()
    m = ice[...].astype(F32)
    drag = jnp.zeros((8, 128), F32)
    for i in range(8):
        drag = jnp.where(cls[...] == i, table[i], drag)

    def plane(p):
        if p < 40:
            return vel[p // L, p % L] * m
        return (drive[0] * m, drive[1] * m, 0.5 * stiff[...] * m, thick[...], drag * m)[p - 40]

    for j in range(STRIPS):
        packed = jnp.zeros((8, 128), F32)
        for g in range(4):
            p = 4 * j + g
            if p < PLANES:
                tile = pltpu.roll(plane(p), 4, 0)
                main[p] = tile
                moved = pltpu.roll(tile, (32 * g + 16) % 128, 1)
                packed = jnp.where((lane >= 32 * g) & (lane < 32 * g + 32), moved, packed)
        strips[j] = packed


def neighbours(tiles, sub, lane):
    n = len(tiles[0])
    rows, cols = [], []
    for lt in range(len(tiles)):
        r, c = [], []
        for k in range(n):
            here = tiles[lt][k]
            up = pltpu.roll(jnp.where(sub == 7, tiles[lt][(k - 1) % n], here), 1, 0)
            dn = pltpu.roll(jnp.where(sub == 0, tiles[lt][(k + 1) % n], here), 7, 0)
            r.append((up, dn))
            if len(tiles) == 2:
                other = tiles[1 - lt][k]
                lf = pltpu.roll(jnp.where(lane == 127, other, here), 1, 1)
                rt = pltpu.roll(jnp.where(lane == 0, other, here), 127, 1)
            else:
                lf = pltpu.roll(here, 1, 1)
                rt = pltpu.roll(here, 127, 1)
            c.append((lf, rt))
        rows.append(r)
        cols.append(c)
    return rows, cols


def weighted(component, row_pair, col_pair):
    a = row_pair[0] + row_pair[1]
    b = col_pair[0] + col_pair[1]
    return 4.0 * a + b if component == 0 else a + 4.0 * b


def main_kernel(
    parity, gm2, swap_b, g0, swap_a, gp2, restrict, expand, vel_out, res_out,
    V, F, Q, E, W, D, C, I, T, X, CA, CB, CE, CF, CX, CQ, CW, CC, CI, CT, PC,
):
    sub, lane = iotas()
    low = sub < 4
    odd = parity[0] == 1
    inner = (lane < 16) | (lane >= 112)

    def from_all(p):
        a, b = swap_a[p], swap_b[p]
        return gm2[p], jnp.where(odd, a, b), g0[p], jnp.where(odd, b, a), gp2[p]

    rims = [from_all(PLANES + j) for j in range(STRIPS)]
    for p in range(PLANES):
        whole = from_all(p)
        j, g = p // 4, p % 4
        for k in range(5):
            main = jnp.where(low, whole[k], whole[(k + 1) % 5])
            rim = jnp.where(low, rims[j][k], rims[j][(k + 1) % 5])
            rim = pltpu.roll(rim, 128 - (32 * g + 16), 1)
            rim = jnp.where(inner, rim, 0.0)
            for lt, tile in ((0, main), (1, rim)):
                if p < 40:
                    V[p, lt, 8 * k : 8 * k + 8, :] = tile
                else:
                    if p == 43:
                        tile = jnp.where(tile > 0.0, tile, 1.0)
                    F[p - 40, lt, 8 * k : 8 * k + 8, :] = tile

    def rows(k):
        return slice(8 * k, 8 * k + 8)

    root = [[jnp.sqrt(F[2, lt, rows(k), :]) for k in range(5)] for lt in range(2)]
    quarter = [[25.0 / (F[3, lt, rows(k), :] * F[3, lt, rows(k), :]) for k in range(5)] for lt in range(2)]
    for lt in range(2):
        for k in range(5):
            T[0, lt, rows(k), :] = root[lt][k]
            T[1, lt, rows(k), :] = quarter[lt][k]

    def visc(z, _):
        after, before = jnp.minimum(z + 1, L - 1), jnp.maximum(z - 1, 0)
        u = [[V[z, lt, rows(k), :] for k in range(5)] for lt in range(2)]
        ur, uc = neighbours(u, sub, lane)
        ux = [[ur[lt][k][1] - ur[lt][k][0] for k in range(5)] for lt in range(2)]
        uy = [[uc[lt][k][1] - uc[lt][k][0] for k in range(5)] for lt in range(2)]
        v = [[V[z + L, lt, rows(k), :] for k in range(5)] for lt in range(2)]
        vr, vc = neighbours(v, sub, lane)
        for lt in range(2):
            for k in range(5):
                vx = vr[lt][k][1] - vr[lt][k][0]
                vy = vc[lt][k][1] - vc[lt][k][0]
                uz = V[after, lt, rows(k), :] - V[before, lt, rows(k), :]
                vz = V[after + L, lt, rows(k), :] - V[before + L, lt, rows(k), :]
                x, y = ux[lt][k], uy[lt][k]
                shear = y + vx
                plane = x * x + vy * vy + x * vy + 0.25 * (shear * shear)
                eps = 0.25 * plane + T[1, lt, rows(k), :] * (uz * uz + vz * vz) + 0.01
                q = T[0, lt, rows(k), :] * jnp.exp(jnp.log(eps) * (-1.0 / 6.0))
                Q[z, lt, rows(k), :] = q
                if k < 4:
                    E[z, lt, rows(k), :] = q * q
        return 0

    lax.fori_loop(0, L, visc, 0, unroll=UNROLL)

    def factor(z, carry):
        top = jnp.where(z < L - 1, 1.0, 0.0)
        bed = jnp.where(z == 0, 1.0, 0.0)
        after = jnp.minimum(z + 1, L - 1)
        q = [[Q[z, lt, rows(k), :] for k in range(5)] for lt in range(2)]
        qr, qc = neighbours(q, sub, lane)
        out = []
        for lt in range(2):
            for k in range(4):
                i = lt * 4 + k
                wbefore, cx, cy = carry[3 * i : 3 * i + 3]
                h = F[3, lt, rows(k), :]
                ih = 20.0 / h
                w = (E[z, lt, rows(k), :] + E[after, lt, rows(k), :]) * (0.5 * top * (ih * ih))
                off = jnp.where(F[2, lt, rows(k), :] > 0.0, 0.0, 1.0)
                common = w + wbefore + bed * (F[4, lt, rows(k), :] * ih) + off
                W[z, lt, rows(k), :] = w
                new = [w]
                for component, cb in ((0, cx), (1, cy)):
                    d = q[lt][k] * weighted(component, qr[lt][k], qc[lt][k]) + common
                    inv = 1.0 / (d - wbefore * cb)
                    c = w * inv
                    D[component * L + z, lt, rows(k), :] = d
                    I[component * L + z, lt, rows(k), :] = inv
                    C[component * L + z, lt, rows(k), :] = c
                    new.append(c)
                out += new
        return tuple(out)

    zero = jnp.zeros((8, 128), F32)
    lax.fori_loop(0, L, factor, (zero,) * 24, unroll=UNROLL)

    def forward(src, tiles, rim_tile):
        n = len(tiles)
        use = tiles + ([rim_tile] if rim_tile is not None else [])

        def step(z, carry):
            out = []
            for component in range(2):
                p = component * L + z
                q = [[Q[z, lt, rows(k), :] for k in use] for lt in range(2)]
                y = [[q[lt][i] * src[p, lt, rows(k), :] for i, k in enumerate(use)] for lt in range(2)]
                yr, yc = neighbours(y, sub, lane)
                for lt in range(2):
                    for i, k in enumerate(tiles):
                        t = F[component, lt, rows(k), :] + q[lt][i] * weighted(component, yr[lt][i], yc[lt][i])
                        t = t + carry[(component * 2 + lt) * n + i]
                        T[p, lt, rows(k), :] = t
                        out.append(C[p, lt, rows(k), :] * t)
            return tuple(out)

        lax.fori_loop(0, L, step, (zero,) * (4 * n), unroll=UNROLL)

    def backward(src, dst, tiles):
        n = len(tiles)

        def step(s, carry):
            z = L - 1 - s
            out = []
            for component in range(2):
                p = component * L + z
                for lt in range(2):
                    for i, k in enumerate(tiles):
                        new = I[p, lt, rows(k), :] * T[p, lt, rows(k), :] + C[p, lt, rows(k), :] * carry[(component * 2 + lt) * n + i]
                        dst[p, lt, rows(k), :] = 0.2 * src[p, lt, rows(k), :] + 0.8 * new
                        out.append(new)
            return tuple(out)

        lax.fori_loop(0, L, step, (zero,) * (4 * n), unroll=UNROLL)

    def remainder(src, tiles, put):
        n = len(tiles)

        def step(z, carry):
            after = jnp.minimum(z + 1, L - 1)
            out = []
            for component in range(2):
                p = component * L + z
                x = [[src[p, lt, rows(k), :] for k in tiles] for lt in range(2)]
                q = [[Q[z, lt, rows(k), :] for k in tiles] for lt in range(2)]
                y = [[q[lt][i] * x[lt][i] for i in range(n)] for lt in range(2)]
                yr, yc = neighbours(y, sub, lane)
                got = []
                for lt in range(2):
                    for i, k in enumerate(tiles):
                        w = W[z, lt, rows(k), :]
                        r = F[component, lt, rows(k), :] + q[lt][i] * weighted(component, yr[lt][i], yc[lt][i])
                        r = r - D[p, lt, rows(k), :] * x[lt][i]
                        r = r + w * src[after + component * L, lt, rows(k), :] + carry[(component * 2 + lt) * n + i]
                        got.append(r)
                        out.append(w * x[lt][i])
                put(component, z, got)
            return tuple(out)

        lax.fori_loop(0, L, step, (zero,) * (4 * n), unroll=UNROLL)

    pre = [0, 1, 2, 3]
    forward(V, pre, 4)
    backward(V, X, pre)
    forward(X, pre, None)
    backward(X, X, pre)

    def put_rem(component, z, got):
        for lt in range(2):
            for i, k in enumerate(pre):
                T[component * L + z, lt, rows(k), :] = got[lt * 4 + i]

    remainder(X, pre, put_rem)

    even, odd = pl.ds(0, 16, stride=2), pl.ds(1, 16, stride=2)

    def gather(p, _):
        for lt in range(2):
            CA[lt, pl.ds(pl.multiple_of(p * 16, 16), 16), :] = T[p, lt, even, :] + T[p, lt, odd, :]
        return 0

    lax.fori_loop(0, 40, gather, 0, unroll=UNROLL)

    def gather_eta(z, _):
        for lt in range(2):
            CA[lt, pl.ds(pl.multiple_of((z + 40) * 16, 16), 16), :] = E[z, lt, even, :] + E[z, lt, odd, :]
        return 0

    lax.fori_loop(0, L, gather_eta, 0, unroll=UNROLL)
    for i in range(3):
        for lt in range(2):
            CA[lt, (60 + i) * 16 : (61 + i) * 16, :] = F[2 + i, lt, even, :] + F[2 + i, lt, odd, :]
    CB[...] = jnp.dot(
        CA[0], restrict[0], precision=lax.Precision.HIGHEST, preferred_element_type=F32
    ) + jnp.dot(CA[1], restrict[1], precision=lax.Precision.HIGHEST, preferred_element_type=F32)

    cmask = [jnp.where(CB[960 + 8 * k : 968 + 8 * k, :] > 0.0, 0.0, 1.0) for k in range(2)]
    cthick = [CB[976 + 8 * k : 984 + 8 * k, :] for k in range(2)]
    cih = [20.0 / jnp.where(t > 0.0, t, 1.0) for t in cthick]
    cdrag = [CB[992 + 8 * k : 1000 + 8 * k, :] * cih[k] for k in range(2)]

    def at(p, k):
        return pl.ds(pl.multiple_of(p * 16 + 8 * k, 8), 8)

    def coarse_factor(z, carry):
        top = jnp.where(z < L - 1, 1.0, 0.0)
        bed = jnp.where(z == 0, 1.0, 0.0)
        after = jnp.minimum(z + 1, L - 1)
        e = [CB[at(40 + z, k), :] for k in range(2)]
        q = [[0.5 * jnp.sqrt(e[k]) for k in range(2)]]
        qr, qc = neighbours(q, sub, lane)
        out = []
        for k in range(2):
            wbefore, cx, cy = carry[3 * k : 3 * k + 3]
            w = (e[k] + CB[at(40 + after, k), :]) * (0.5 * top * (cih[k] * cih[k]))
            common = w + wbefore + bed * cdrag[k] + cmask[k]
            CQ[at(z, k), :] = q[0][k]
            new = [w]
            for component, cb in ((0, cx), (1, cy)):
                d = q[0][k] * weighted(component, qr[0][k], qc[0][k]) + common
                inv = 1.0 / (d - wbefore * cb)
                c = w * inv
                CI[at(component * L + z, k), :] = inv
                CC[at(component * L + z, k), :] = c
                new.append(c)
            out += new
        return tuple(out)

    lax.fori_loop(0, L, coarse_factor, (zero,) * 6, unroll=UNROLL)

    for turn in range(4):

        def coarse_forward(z, carry, turn=turn):
            out = []
            for component in range(2):
                p = component * L + z
                if turn > 0:
                    q = [CQ[at(z, k), :] for k in range(2)]
                    y = [[q[k] * CX[at(p, k), :] for k in range(2)]]
                    yr, yc = neighbours(y, sub, lane)
                for k in range(2):
                    t = CB[at(p, k), :] + carry[component * 2 + k]
                    if turn > 0:
                        t = t + q[k] * weighted(component, yr[0][k], yc[0][k])
                    CT[at(p, k), :] = t
                    out.append(CC[at(p, k), :] * t)
            return tuple(out)

        lax.fori_loop(0, L, coarse_forward, (zero,) * 4, unroll=UNROLL)

        def coarse_backward(s, carry, turn=turn):
            z = L - 1 - s
            out = []
            for component in range(2):
                p = component * L + z
                for k in range(2):
                    new = CI[at(p, k), :] * CT[at(p, k), :] + CC[at(p, k), :] * carry[component * 2 + k]
                    if turn > 0:
                        CX[at(p, k), :] = 0.2 * CX[at(p, k), :] + 0.8 * new
                    else:
                        CX[at(p, k), :] = 0.8 * new
                    out.append(new)
            return tuple(out)

        lax.fori_loop(0, L, coarse_backward, (zero,) * 4, unroll=UNROLL)

    def spread(p, _):
        CE[pl.ds(pl.multiple_of(p * 8, 8), 8), :] = pltpu.roll(
            jnp.where(low, CX[at(p, 1), :], CX[at(p, 0), :]), 4, 0
        )
        return 0

    lax.fori_loop(0, 40, spread, 0, unroll=UNROLL)
    for lt in range(2):
        CF[lt] = jnp.dot(CE[...], expand[lt], precision=lax.Precision.HIGHEST, preferred_element_type=F32)

    def correct(p, _):
        for lt in range(2):
            tile = CF[lt, pl.ds(pl.multiple_of(p * 8, 8), 8), :]
            PC[p, lt, pl.ds(0, 8, stride=2), :] = tile
            PC[p, lt, pl.ds(1, 8, stride=2), :] = tile
            for k in (1, 2):
                m = jnp.where(F[2, lt, rows(k), :] > 0.0, 1.0, 0.0)
                X[p, lt, rows(k), :] = X[p, lt, rows(k), :] + m * PC[p, lt, rows(k - 1), :]
        return 0

    lax.fori_loop(0, 40, correct, 0, unroll=UNROLL)

    post = [1, 2]
    for _ in range(2):
        forward(X, post, None)
        backward(X, X, post)

    def put_res(component, z, got):
        res_out[component, z] = pltpu.roll(jnp.where(low, got[1], got[0]), 4, 0)
        p = component * L + z
        vel_out[component, z] = pltpu.roll(jnp.where(low, X[p, 0, rows(2), :], X[p, 0, rows(1), :]), 4, 0)

    remainder(X, post, put_res)


def transfer_matrices():
    lane = jnp.arange(128)
    main = lane // 2
    rim = jnp.where(lane < 16, 64 + lane // 2, jnp.where(lane >= 112, 120 + (lane - 112) // 2, -1))
    hits = jnp.stack([main, rim])[:, :, None] == lane[None, None, :]
    restrict = jnp.where(hits, 0.25, 0.0).astype(F32)
    expand = jnp.where(hits, 1.0, 0.0).astype(F32).transpose(0, 2, 1)
    return restrict, expand


def pairs(move):
    def of(axis):
        rows, cols = lax.axis_size("gx"), lax.axis_size("gy")
        count = rows if axis == "gx" else cols
        hops = [(i, move(i)) for i in range(count) if 0 <= move(i) < count]
        if axis == "gx":
            return [(i * cols + j, k * cols + j) for i, k in hops for j in range(cols)]
        return [(i * cols + j, i * cols + k) for i in range(rows) for j, k in hops]

    return of


def send(cells, axis, move):
    return lax.ppermute(cells, ("gx", "gy"), pairs(move)(axis))


def inner_swap(i):
    return i ^ 1


def outer_swap(i):
    return ((i + 1) ^ 1) - 1


def per_device(velocity, drive, stiffness, thickness, ice_mask, friction_class, friction_table):
    vmem = pl.BlockSpec(memory_space=pltpu.VMEM)
    smem = pl.BlockSpec(memory_space=pltpu.SMEM)
    main, strips = pl.pallas_call(
        pack_kernel,
        out_shape=(jax.ShapeDtypeStruct((PLANES, 8, 128), F32), jax.ShapeDtypeStruct((STRIPS, 8, 128), F32)),
        in_specs=[vmem] * 6 + [smem],
        out_specs=(vmem, vmem),
        name="pack",
    )(velocity, drive, stiffness, thickness, ice_mask, friction_class, friction_table)
    inner = send(strips, "gy", inner_swap)
    outer = send(strips, "gy", outer_swap)
    odd = lax.axis_index("gy") % 2 == 1
    left = jnp.where(odd, inner, outer)
    right = jnp.where(odd, outer, inner)
    lane = lax.broadcasted_iota(jnp.int32, strips.shape, 2)
    rim = jnp.where(lane % 32 < 16, left, right)
    whole = jnp.concatenate([main, rim], axis=0)
    before = send(whole, "gx", lambda i: i + 2)
    after = send(whole, "gx", lambda i: i - 2)
    outer = send(whole, "gx", outer_swap)
    inner = send(whole, "gx", inner_swap)
    parity = (lax.axis_index("gx") % 2).astype(jnp.int32).reshape(1)
    parts = (parity, before, outer, whole, inner, after)
    restrict, expand = transfer_matrices()
    fine = lambda n, r: pltpu.VMEM((n, 2, r, 128), F32)
    coarse = lambda n: pltpu.VMEM((16 * n, 128), F32)
    out = jax.ShapeDtypeStruct((2, L, 8, 128), F32)
    return pl.pallas_call(
        main_kernel,
        out_shape=(out, out),
        in_specs=[smem] + [vmem] * 7,
        out_specs=(vmem, vmem),
        scratch_shapes=[
            fine(40, 40), fine(5, 40), fine(20, 40), fine(20, 32), fine(20, 32), fine(40, 32), fine(40, 32), fine(40, 32),
            fine(40, 40), fine(40, 32),
            pltpu.VMEM((2, 63 * 16, 128), F32), coarse(63), pltpu.VMEM((320, 128), F32), pltpu.VMEM((2, 320, 128), F32),
            coarse(40), coarse(20), coarse(20), coarse(40), coarse(40), coarse(40), fine(40, 16),
        ],
        compiler_params=pltpu.CompilerParams(vmem_limit_bytes=48 * 1024 * 1024),
        name="cycle",
    )(*parts, restrict, expand)


def solution(mesh):
    return jax.shard_map(
        per_device,
        mesh=mesh,
        in_specs=(
            P(None, None, "gx", "gy"),
            P(None, "gx", "gy"),
            P("gx", "gy"),
            P("gx", "gy"),
            P("gx", "gy"),
            P("gx", "gy"),
            P(),
        ),
        out_specs=(P(None, None, "gx", "gy"), P(None, None, "gx", "gy")),
        check_vma=False,
    )
```

```python
import jax
import jax.numpy as jnp
from jax import lax
from jax.experimental import pallas as pl
from jax.experimental.pallas import tpu as pltpu
from jax.sharding import PartitionSpec as P

L = 20
PLANES = 45
STRIPS = 12
F32 = jnp.float32
UNROLL = 20


def iotas(shape=(8, 128)):
    return lax.broadcasted_iota(jnp.int32, shape, 0), lax.broadcasted_iota(jnp.int32, shape, 1)


def pack_kernel(vel, drive, stiff, thick, ice, cls, table, main, strips):
    sub, lane = iotas()
    m = ice[...].astype(F32)
    drag = jnp.zeros((8, 128), F32)
    for i in range(8):
        drag = jnp.where(cls[...] == i, table[i], drag)

    def plane(p):
        if p < 40:
            return vel[p // L, p % L] * m
        return (drive[0] * m, drive[1] * m, 0.5 * stiff[...] * m, thick[...], drag * m)[p - 40]

    for j in range(STRIPS):
        packed = jnp.zeros((8, 128), F32)
        for g in range(4):
            p = 4 * j + g
            if p < PLANES:
                tile = pltpu.roll(plane(p), 4, 0)
                main[p] = tile
                moved = pltpu.roll(tile, (32 * g + 16) % 128, 1)
                packed = jnp.where((lane >= 32 * g) & (lane < 32 * g + 32), moved, packed)
        strips[j] = packed


def beside(tiles, lane):
    out = []
    for lt, row in enumerate(tiles):
        pairs_ = []
        for k, here in enumerate(row):
            other = tiles[lt - 1][k]
            before = here if len(tiles) == 1 else jnp.where(lane == 127, other, here)
            after = here if len(tiles) == 1 else jnp.where(lane == 0, other, here)
            pairs_.append((pltpu.roll(before, 1, 1), pltpu.roll(after, 127, 1)))
        out.append(pairs_)
    return out


def weighted(component, row_pair, col_pair):
    a = row_pair[0] + row_pair[1]
    b = col_pair[0] + col_pair[1]
    return 4.0 * a + b if component == 0 else a + 4.0 * b


def product(values, weights):
    first = values.astype(jnp.bfloat16)
    second = (values - first.astype(F32)).astype(jnp.bfloat16)
    return jnp.dot(jnp.concatenate([first, second], axis=1), weights, preferred_element_type=F32)


def main_kernel(
    parity, gm2, swap_b, g0, swap_a, gp2, restrict, expand, vel_out, res_out,
    V, F, Q, R, E, W, FS, D, C, I, T, X, CA, CB, CE, CF, CX, CQ, CR, CC, CI, CT, PC,
):
    sub, lane = iotas()
    low = sub < 4
    odd = parity[0] == 1
    inner = (lane < 16) | (lane >= 112)

    def from_all(p):
        a, b = swap_a[p], swap_b[p]
        return gm2[p], jnp.where(odd, a, b), g0[p], jnp.where(odd, b, a), gp2[p]

    rims = [from_all(PLANES + j) for j in range(STRIPS)]
    for p in range(PLANES):
        whole = from_all(p)
        j, g = p // 4, p % 4
        for k in range(5):
            main = jnp.where(low, whole[k], whole[(k + 1) % 5])
            rim = jnp.where(low, rims[j][k], rims[j][(k + 1) % 5])
            rim = pltpu.roll(rim, 128 - (32 * g + 16), 1)
            rim = jnp.where(inner, rim, 0.0)
            for lt, tile in ((0, main), (1, rim)):
                if p < 40:
                    V[p, lt, 8 * k + 8 : 8 * k + 16, :] = tile
                    if k == 4:
                        V[p, lt, 0:8, :] = tile
                    if k == 0:
                        V[p, lt, 48:56, :] = tile
                else:
                    if p == 43:
                        tile = jnp.where(tile > 0.0, tile, 1.0)
                    F[p - 40, lt, 8 * k : 8 * k + 8, :] = tile

    def rows(k):
        return slice(8 * k, 8 * k + 8)

    def inside(k):
        return slice(8 * k + 8, 8 * k + 16)

    def around(ref, p, tiles):
        here = [[ref[p, lt, inside(k), :] for k in tiles] for lt in range(2)]
        up_down = [[(ref[p, lt, pl.ds(8 * k + 7, 8), :], ref[p, lt, pl.ds(8 * k + 9, 8), :]) for k in tiles] for lt in range(2)]
        return here, up_down, beside(here, lane)

    root = [[jnp.sqrt(F[2, lt, rows(k), :]) for k in range(5)] for lt in range(2)]
    quarter = [[25.0 / (F[3, lt, rows(k), :] * F[3, lt, rows(k), :]) for k in range(5)] for lt in range(2)]
    for lt in range(2):
        for k in range(5):
            T[0, lt, rows(k), :] = root[lt][k]
            T[1, lt, rows(k), :] = quarter[lt][k]
            T[2, lt, rows(k), :] = jnp.where(root[lt][k] > 0.0, 1.0 / root[lt][k], 0.0)

    def visc(z, _):
        after, before = jnp.minimum(z + 1, L - 1), jnp.maximum(z - 1, 0)
        u, ur, uc = around(V, z, range(5))
        ux = [[ur[lt][k][1] - ur[lt][k][0] for k in range(5)] for lt in range(2)]
        uy = [[uc[lt][k][1] - uc[lt][k][0] for k in range(5)] for lt in range(2)]
        v, vr, vc = around(V, z + L, range(5))
        for lt in range(2):
            for k in range(5):
                vx = vr[lt][k][1] - vr[lt][k][0]
                vy = vc[lt][k][1] - vc[lt][k][0]
                uz = V[after, lt, inside(k), :] - V[before, lt, inside(k), :]
                vz = V[after + L, lt, inside(k), :] - V[before + L, lt, inside(k), :]
                x, y = ux[lt][k], uy[lt][k]
                shear = y + vx
                plane = x * x + vy * vy + x * vy + 0.25 * (shear * shear)
                eps = 0.25 * plane + T[1, lt, rows(k), :] * (uz * uz + vz * vz) + 0.01
                sixth = jnp.log(eps) * (1.0 / 6.0)
                q = T[0, lt, rows(k), :] * jnp.exp(-sixth)
                for place in (inside(k), slice(0, 8))[: 2 if k == 4 else 1]:
                    Q[z, lt, place, :] = q
                    X[z, lt, place, :] = q * u[lt][k]
                    X[z + L, lt, place, :] = q * v[lt][k]
                if k < 4:
                    back = T[2, lt, rows(k), :] * jnp.exp(sixth)
                    R[z, lt, rows(k), :] = back
                    E[z, lt, rows(k), :] = q * q
                    FS[z, lt, rows(k), :] = F[0, lt, rows(k), :] * back
                    FS[z + L, lt, rows(k), :] = F[1, lt, rows(k), :] * back
        return 0

    lax.fori_loop(0, L, visc, 0, unroll=UNROLL)

    def factor(z, carry):
        top = jnp.where(z < L - 1, 1.0, 0.0)
        bed = jnp.where(z == 0, 1.0, 0.0)
        after = jnp.minimum(z + 1, L - 1)
        q, qr, qc = around(Q, z, range(4))
        out = []
        for lt in range(2):
            for k in range(4):
                i = lt * 4 + k
                wbefore, sbefore, cx, cy = carry[4 * i : 4 * i + 4]
                ice = F[2, lt, rows(k), :] > 0.0
                ih = 20.0 / F[3, lt, rows(k), :]
                back = R[z, lt, rows(k), :]
                w = (E[z, lt, rows(k), :] + E[after, lt, rows(k), :]) * (0.5 * top * (ih * ih))
                scaled = w * (back * R[after, lt, rows(k), :])
                common = (w + wbefore + bed * (F[4, lt, rows(k), :] * ih)) * (back * back)
                off = jnp.where(ice, 0.0, 1.0)
                share = jnp.where(ice, 0.8, 0.0)
                W[z, lt, rows(k), :] = scaled
                new = [w, scaled]
                for component, cb in ((0, cx), (1, cy)):
                    d = back * weighted(component, qr[lt][k], qc[lt][k]) + common
                    inv = 1.0 / (d + off - sbefore * cb)
                    c = scaled * inv
                    D[component * L + z, lt, rows(k), :] = d
                    I[component * L + z, lt, rows(k), :] = share * inv
                    C[component * L + z, lt, rows(k), :] = c
                    new.append(c)
                out += new
        return tuple(out)

    zero = jnp.zeros((8, 128), F32)
    lax.fori_loop(0, L, factor, (zero,) * 32, unroll=UNROLL)

    def forward(tiles):
        n = len(tiles)

        def step(z, carry):
            out = []
            for component in range(2):
                p = component * L + z
                y, yr, yc = around(X, p, tiles)
                for lt in range(2):
                    for i, k in enumerate(tiles):
                        t = FS[p, lt, rows(k), :] + weighted(component, yr[lt][i], yc[lt][i])
                        t = t + carry[(component * 2 + lt) * n + i]
                        T[p, lt, rows(k), :] = t
                        out.append(C[p, lt, rows(k), :] * t)
            return tuple(out)

        lax.fori_loop(0, L, step, (zero,) * (4 * n), unroll=UNROLL)

    def backward(tiles):
        n = len(tiles)

        def step(s, carry):
            z = L - 1 - s
            out = []
            for component in range(2):
                p = component * L + z
                for lt in range(2):
                    for i, k in enumerate(tiles):
                        new = I[p, lt, rows(k), :] * T[p, lt, rows(k), :] + C[p, lt, rows(k), :] * carry[(component * 2 + lt) * n + i]
                        X[p, lt, inside(k), :] = 0.2 * X[p, lt, inside(k), :] + new
                        out.append(new)
            return tuple(out)

        lax.fori_loop(0, L, step, (zero,) * (4 * n), unroll=UNROLL)

    def remainder(tiles, put):
        n = len(tiles)

        def step(z, carry):
            after = jnp.minimum(z + 1, L - 1)
            out = []
            for component in range(2):
                p = component * L + z
                y, yr, yc = around(X, p, tiles)
                got = []
                for lt in range(2):
                    for i, k in enumerate(tiles):
                        w = W[z, lt, rows(k), :]
                        r = FS[p, lt, rows(k), :] + weighted(component, yr[lt][i], yc[lt][i])
                        r = r - D[p, lt, rows(k), :] * y[lt][i]
                        r = r + w * X[after + component * L, lt, inside(k), :] + carry[(component * 2 + lt) * n + i]
                        got.append(Q[z, lt, inside(k), :] * r)
                        out.append(w * y[lt][i])
                put(component, z, got)
            return tuple(out)

        lax.fori_loop(0, L, step, (zero,) * (4 * n), unroll=UNROLL)

    pre = [0, 1, 2, 3]
    forward(pre)
    backward(pre)
    forward(pre)
    backward(pre)

    def put_rem(component, z, got):
        for lt in range(2):
            for i, k in enumerate(pre):
                T[component * L + z, lt, rows(k), :] = got[lt * 4 + i]

    remainder(pre, put_rem)

    even, odd = pl.ds(0, 16, stride=2), pl.ds(1, 16, stride=2)

    def gather(p, _):
        for lt in range(2):
            CA[lt, pl.ds(pl.multiple_of(p * 16, 16), 16), :] = T[p, lt, even, :] + T[p, lt, odd, :]
        return 0

    lax.fori_loop(0, 40, gather, 0, unroll=UNROLL)

    def gather_eta(z, _):
        for lt in range(2):
            CA[lt, pl.ds(pl.multiple_of((z + 40) * 16, 16), 16), :] = E[z, lt, even, :] + E[z, lt, odd, :]
        return 0

    lax.fori_loop(0, L, gather_eta, 0, unroll=UNROLL)
    for i in range(3):
        for lt in range(2):
            CA[lt, (60 + i) * 16 : (61 + i) * 16, :] = F[2 + i, lt, even, :] + F[2 + i, lt, odd, :]
    CB[...] = product(CA[0], restrict[0]) + product(CA[1], restrict[1])

    cmask = [jnp.where(CB[960 + 8 * k : 968 + 8 * k, :] > 0.0, 0.0, 1.0) for k in range(2)]
    cthick = [CB[976 + 8 * k : 984 + 8 * k, :] for k in range(2)]
    cih = [20.0 / jnp.where(t > 0.0, t, 1.0) for t in cthick]
    cdrag = [CB[992 + 8 * k : 1000 + 8 * k, :] * cih[k] for k in range(2)]

    def padded(p, k, by=0):
        return pl.ds(p * 16 + 8 * k + 8 + by, 8)

    def coarse_around(ref, p):
        here = [ref[padded(p, k), :] for k in range(2)]
        up_down = [(ref[padded(p, k, -1), :], ref[padded(p, k, 1), :]) for k in range(2)]
        return up_down, beside([here], lane)[0]

    for ref, size in ((CX, 40), (CQ, 20)):
        ref[0:8, :] = zero
        ref[16 * size + 8 : 16 * size + 16, :] = zero

    def at(p, k):
        return pl.ds(pl.multiple_of(p * 16 + 8 * k, 8), 8)

    def coarse_roots(z, _):
        for k in range(2):
            e = CB[at(40 + z, k), :]
            q = 0.5 * jnp.sqrt(e)
            back = jnp.where(e > 0.0, 1.0 / q, 0.0)
            CQ[padded(z, k), :] = q
            CR[at(z, k), :] = back
            for component in range(2):
                CB[at(component * L + z, k), :] = CB[at(component * L + z, k), :] * back
        return 0

    lax.fori_loop(0, L, coarse_roots, 0, unroll=UNROLL)

    def coarse_factor(z, carry):
        top = jnp.where(z < L - 1, 1.0, 0.0)
        bed = jnp.where(z == 0, 1.0, 0.0)
        after = jnp.minimum(z + 1, L - 1)
        qr, qc = coarse_around(CQ, z)
        out = []
        for k in range(2):
            wbefore, sbefore, cx, cy = carry[4 * k : 4 * k + 4]
            back = CR[at(z, k), :]
            w = (CB[at(40 + z, k), :] + CB[at(40 + after, k), :]) * (0.5 * top * (cih[k] * cih[k]))
            scaled = w * (back * CR[at(after, k), :])
            common = (w + wbefore + bed * cdrag[k]) * (back * back)
            new = [w, scaled]
            for component, cb in ((0, cx), (1, cy)):
                d = back * weighted(component, qr[k], qc[k]) + common
                inv = 1.0 / (d + cmask[k] - sbefore * cb)
                c = scaled * inv
                CI[at(component * L + z, k), :] = (0.8 - 0.8 * cmask[k]) * inv
                CC[at(component * L + z, k), :] = c
                new.append(c)
            out += new
        return tuple(out)

    lax.fori_loop(0, L, coarse_factor, (zero,) * 8, unroll=UNROLL)

    for turn in range(4):

        def coarse_forward(z, carry, turn=turn):
            out = []
            for component in range(2):
                p = component * L + z
                if turn > 0:
                    yr, yc = coarse_around(CX, p)
                for k in range(2):
                    t = CB[at(p, k), :] + carry[component * 2 + k]
                    if turn > 0:
                        t = t + weighted(component, yr[k], yc[k])
                    CT[at(p, k), :] = t
                    out.append(CC[at(p, k), :] * t)
            return tuple(out)

        lax.fori_loop(0, L, coarse_forward, (zero,) * 4, unroll=UNROLL)

        def coarse_backward(s, carry, turn=turn):
            z = L - 1 - s
            out = []
            for component in range(2):
                p = component * L + z
                for k in range(2):
                    new = CI[at(p, k), :] * CT[at(p, k), :] + CC[at(p, k), :] * carry[component * 2 + k]
                    if turn > 0:
                        CX[padded(p, k), :] = 0.2 * CX[padded(p, k), :] + new
                    else:
                        CX[padded(p, k), :] = new
                    out.append(new)
            return tuple(out)

        lax.fori_loop(0, L, coarse_backward, (zero,) * 4, unroll=UNROLL)

    def spread(p, _):
        CE[pl.ds(pl.multiple_of(p * 8, 8), 8), :] = pltpu.roll(
            jnp.where(low, CX[padded(p, 1), :] * CR[at(lax.rem(p, L), 1), :], CX[padded(p, 0), :] * CR[at(lax.rem(p, L), 0), :]), 4, 0
        )
        return 0

    lax.fori_loop(0, 40, spread, 0, unroll=UNROLL)
    for lt in range(2):
        CF[lt] = product(CE[...], expand[lt])

    def correct(p, _):
        for lt in range(2):
            tile = CF[lt, pl.ds(pl.multiple_of(p * 8, 8), 8), :]
            PC[p, lt, pl.ds(0, 8, stride=2), :] = tile
            PC[p, lt, pl.ds(1, 8, stride=2), :] = tile
            for k in (1, 2):
                q = Q[lax.rem(p, L), lt, inside(k), :]
                X[p, lt, inside(k), :] = X[p, lt, inside(k), :] + q * PC[p, lt, rows(k - 1), :]
        return 0

    lax.fori_loop(0, 40, correct, 0, unroll=UNROLL)

    post = [1, 2]
    for _ in range(2):
        forward(post)
        backward(post)

    def put_res(component, z, got):
        res_out[component, z] = pltpu.roll(jnp.where(low, got[1], got[0]), 4, 0)
        p = component * L + z
        vel = [X[p, 0, inside(k), :] * R[z, 0, rows(k), :] for k in (1, 2)]
        vel_out[component, z] = pltpu.roll(jnp.where(low, vel[1], vel[0]), 4, 0)

    remainder(post, put_res)


def transfer_matrices():
    lane = jnp.arange(128)
    main = lane // 2
    rim = jnp.where(lane < 16, 64 + lane // 2, jnp.where(lane >= 112, 120 + (lane - 112) // 2, -1))
    hits = jnp.stack([main, rim])[:, :, None] == lane[None, None, :]
    restrict = jnp.where(hits, 0.25, 0.0).astype(F32)
    expand = jnp.where(hits, 1.0, 0.0).astype(F32).transpose(0, 2, 1)
    twice = lambda w: jnp.concatenate([w, w], axis=1).astype(jnp.bfloat16)
    return twice(restrict), twice(expand)


def pairs(move):
    def of(axis):
        rows, cols = lax.axis_size("gx"), lax.axis_size("gy")
        count = rows if axis == "gx" else cols
        hops = [(i, move(i)) for i in range(count) if 0 <= move(i) < count]
        if axis == "gx":
            return [(i * cols + j, k * cols + j) for i, k in hops for j in range(cols)]
        return [(i * cols + j, i * cols + k) for i in range(rows) for j, k in hops]

    return of


def send(cells, axis, move):
    return lax.ppermute(cells, ("gx", "gy"), pairs(move)(axis))


def inner_swap(i):
    return i ^ 1


def outer_swap(i):
    return ((i + 1) ^ 1) - 1


def per_device(velocity, drive, stiffness, thickness, ice_mask, friction_class, friction_table):
    vmem = pl.BlockSpec(memory_space=pltpu.VMEM)
    smem = pl.BlockSpec(memory_space=pltpu.SMEM)
    main, strips = pl.pallas_call(
        pack_kernel,
        out_shape=(jax.ShapeDtypeStruct((PLANES, 8, 128), F32), jax.ShapeDtypeStruct((STRIPS, 8, 128), F32)),
        in_specs=[vmem] * 6 + [smem],
        out_specs=(vmem, vmem),
        name="pack",
    )(velocity, drive, stiffness, thickness, ice_mask, friction_class, friction_table)
    inner = send(strips, "gy", inner_swap)
    outer = send(strips, "gy", outer_swap)
    odd = lax.axis_index("gy") % 2 == 1
    left = jnp.where(odd, inner, outer)
    right = jnp.where(odd, outer, inner)
    lane = lax.broadcasted_iota(jnp.int32, strips.shape, 2)
    rim = jnp.where(lane % 32 < 16, left, right)
    whole = jnp.concatenate([main, rim], axis=0)
    before = send(whole, "gx", lambda i: i + 2)
    after = send(whole, "gx", lambda i: i - 2)
    outer = send(whole, "gx", outer_swap)
    inner = send(whole, "gx", inner_swap)
    parity = (lax.axis_index("gx") % 2).astype(jnp.int32).reshape(1)
    parts = (parity, before, outer, whole, inner, after)
    restrict, expand = transfer_matrices()
    fine = lambda n, r: pltpu.VMEM((n, 2, r, 128), F32)
    coarse = lambda n: pltpu.VMEM((16 * n, 128), F32)
    out = jax.ShapeDtypeStruct((2, L, 8, 128), F32)
    return pl.pallas_call(
        main_kernel,
        out_shape=(out, out),
        in_specs=[smem] + [vmem] * 7,
        out_specs=(vmem, vmem),
        scratch_shapes=[
            fine(40, 56), fine(5, 40), fine(20, 48), fine(20, 32), fine(20, 32), fine(20, 32), fine(40, 32), fine(40, 32),
            fine(40, 32), fine(40, 32), fine(40, 40), fine(40, 48),
            pltpu.VMEM((2, 63 * 16, 128), F32), coarse(63), pltpu.VMEM((320, 128), F32), pltpu.VMEM((2, 320, 128), F32),
            coarse(41), coarse(21), coarse(20), coarse(40), coarse(40), coarse(40), fine(40, 16),
        ],
        compiler_params=pltpu.CompilerParams(vmem_limit_bytes=48 * 1024 * 1024),
        name="cycle",
    )(*parts, restrict, expand)


def solution(mesh):
    return jax.shard_map(
        per_device,
        mesh=mesh,
        in_specs=(
            P(None, None, "gx", "gy"),
            P(None, "gx", "gy"),
            P("gx", "gy"),
            P("gx", "gy"),
            P("gx", "gy"),
            P("gx", "gy"),
            P(),
        ),
        out_specs=(P(None, None, "gx", "gy"), P(None, None, "gx", "gy")),
        check_vma=False,
    )
```

```python
import jax
import jax.numpy as jnp
from jax import lax
from jax.experimental import pallas as pl
from jax.experimental.pallas import tpu as pltpu
from jax.sharding import PartitionSpec as P

L = 20
PLANES = 45
STRIPS = 12
F32 = jnp.float32
UNROLL = 20


def iotas(shape=(8, 128)):
    return lax.broadcasted_iota(jnp.int32, shape, 0), lax.broadcasted_iota(jnp.int32, shape, 1)


def pack_kernel(vel, drive, stiff, thick, ice, cls, table, main, strips):
    sub, lane = iotas()
    m = ice[...].astype(F32)
    drag = jnp.zeros((8, 128), F32)
    for i in range(8):
        drag = jnp.where(cls[...] == i, table[i], drag)

    def plane(p):
        if p < 40:
            return vel[p // L, p % L] * m
        return (drive[0] * m, drive[1] * m, 0.5 * stiff[...] * m, thick[...], drag * m)[p - 40]

    for j in range(STRIPS):
        packed = jnp.zeros((8, 128), F32)
        for g in range(4):
            p = 4 * j + g
            if p < PLANES:
                tile = pltpu.roll(plane(p), 4, 0)
                main[p] = tile
                moved = pltpu.roll(tile, (32 * g + 16) % 128, 1)
                packed = jnp.where((lane >= 32 * g) & (lane < 32 * g + 32), moved, packed)
        strips[j] = packed


def beside(tiles, lane):
    out = []
    for lt, row in enumerate(tiles):
        pairs_ = []
        for k, here in enumerate(row):
            other = tiles[lt - 1][k]
            before = here if len(tiles) == 1 else jnp.where(lane == 127, other, here)
            after = here if len(tiles) == 1 else jnp.where(lane == 0, other, here)
            pairs_.append((pltpu.roll(before, 1, 1), pltpu.roll(after, 127, 1)))
        out.append(pairs_)
    return out


def weighted(component, row_pair, col_pair):
    a = row_pair[0] + row_pair[1]
    b = col_pair[0] + col_pair[1]
    return 4.0 * a + b if component == 0 else a + 4.0 * b


def product(values, weights):
    first = values.astype(jnp.bfloat16)
    second = (values - first.astype(F32)).astype(jnp.bfloat16)
    return jnp.dot(jnp.concatenate([first, second], axis=1), weights, preferred_element_type=F32)


def main_kernel(
    parity, gm2, swap_b, g0, swap_a, gp2, restrict, expand, vel_out, res_out,
    V, F, Q, R, E, W, FS, D, C, I, T, X, CA, CB, CE, CF, CX, CQ, CR, CC, CI, CT, PC,
):
    sub, lane = iotas()
    low = sub < 4
    odd = parity[0] == 1
    inner = (lane < 16) | (lane >= 112)

    def from_all(p):
        a, b = swap_a[p], swap_b[p]
        return gm2[p], jnp.where(odd, a, b), g0[p], jnp.where(odd, b, a), gp2[p]

    rims = [from_all(PLANES + j) for j in range(STRIPS)]
    for p in range(PLANES):
        whole = from_all(p)
        j, g = p // 4, p % 4
        for k in range(5):
            main = jnp.where(low, whole[k], whole[(k + 1) % 5])
            rim = jnp.where(low, rims[j][k], rims[j][(k + 1) % 5])
            rim = pltpu.roll(rim, 128 - (32 * g + 16), 1)
            rim = jnp.where(inner, rim, 0.0)
            for lt, tile in ((0, main), (1, rim)):
                if p < 40:
                    V[p, lt, 8 * k + 8 : 8 * k + 16, :] = tile
                    if k == 4:
                        V[p, lt, 0:8, :] = tile
                    if k == 0:
                        V[p, lt, 48:56, :] = tile
                else:
                    if p == 43:
                        tile = jnp.where(tile > 0.0, tile, 1.0)
                    F[p - 40, lt, 8 * k : 8 * k + 8, :] = tile

    def rows(k):
        return slice(8 * k, 8 * k + 8)

    def inside(k):
        return slice(8 * k + 8, 8 * k + 16)

    def around(ref, p, tiles):
        here = [[ref[p, lt, inside(k), :] for k in tiles] for lt in range(2)]
        up_down = [[(ref[p, lt, pl.ds(8 * k + 7, 8), :], ref[p, lt, pl.ds(8 * k + 9, 8), :]) for k in tiles] for lt in range(2)]
        return here, up_down, beside(here, lane)

    root = [[jnp.sqrt(F[2, lt, rows(k), :]) for k in range(5)] for lt in range(2)]
    quarter = [[25.0 / (F[3, lt, rows(k), :] * F[3, lt, rows(k), :]) for k in range(5)] for lt in range(2)]
    for lt in range(2):
        for k in range(5):
            T[0, lt, rows(k), :] = root[lt][k]
            T[1, lt, rows(k), :] = quarter[lt][k]
            T[2, lt, rows(k), :] = jnp.where(root[lt][k] > 0.0, 1.0 / root[lt][k], 0.0)

    def visc(z, _):
        after, before = jnp.minimum(z + 1, L - 1), jnp.maximum(z - 1, 0)
        u, ur, uc = around(V, z, range(5))
        ux = [[ur[lt][k][1] - ur[lt][k][0] for k in range(5)] for lt in range(2)]
        uy = [[uc[lt][k][1] - uc[lt][k][0] for k in range(5)] for lt in range(2)]
        v, vr, vc = around(V, z + L, range(5))
        for lt in range(2):
            for k in range(5 - lt):
                vx = vr[lt][k][1] - vr[lt][k][0]
                vy = vc[lt][k][1] - vc[lt][k][0]
                uz = V[after, lt, inside(k), :] - V[before, lt, inside(k), :]
                vz = V[after + L, lt, inside(k), :] - V[before + L, lt, inside(k), :]
                x, y = ux[lt][k], uy[lt][k]
                shear = y + vx
                plane = x * x + vy * vy + x * vy + 0.25 * (shear * shear)
                eps = 0.25 * plane + T[1, lt, rows(k), :] * (uz * uz + vz * vz) + 0.01
                sixth = jnp.log(eps) * (1.0 / 6.0)
                q = T[0, lt, rows(k), :] * jnp.exp(-sixth)
                for place in (inside(k), slice(0, 8))[: 2 if k == 4 else 1]:
                    Q[z, lt, place, :] = q
                    X[z, lt, place, :] = q * u[lt][k]
                    X[z + L, lt, place, :] = q * v[lt][k]
                if k < 4:
                    back = T[2, lt, rows(k), :] * jnp.exp(sixth)
                    R[z, lt, rows(k), :] = back
                    E[z, lt, rows(k), :] = q * q
                    FS[z, lt, rows(k), :] = F[0, lt, rows(k), :] * back
                    FS[z + L, lt, rows(k), :] = F[1, lt, rows(k), :] * back
        return 0

    lax.fori_loop(0, L, visc, 0, unroll=UNROLL)
    for z in range(L):
        for place in (slice(0, 8), slice(40, 48)):
            for ref, p in ((Q, z), (X, z), (X, z + L)):
                ref[p, 1, place, :] = jnp.zeros((8, 128), F32)

    def factor(z, carry):
        top = jnp.where(z < L - 1, 1.0, 0.0)
        bed = jnp.where(z == 0, 1.0, 0.0)
        after = jnp.minimum(z + 1, L - 1)
        q, qr, qc = around(Q, z, range(4))
        out = []
        for lt in range(2):
            for k in range(4):
                i = lt * 4 + k
                wbefore, sbefore, cx, cy = carry[4 * i : 4 * i + 4]
                ice = F[2, lt, rows(k), :] > 0.0
                ih = 20.0 / F[3, lt, rows(k), :]
                back = R[z, lt, rows(k), :]
                w = (E[z, lt, rows(k), :] + E[after, lt, rows(k), :]) * (0.5 * top * (ih * ih))
                scaled = w * (back * R[after, lt, rows(k), :])
                common = (w + wbefore + bed * (F[4, lt, rows(k), :] * ih)) * (back * back)
                off = jnp.where(ice, 0.0, 1.0)
                share = jnp.where(ice, 0.8, 0.0)
                W[z, lt, rows(k), :] = scaled
                new = [w, scaled]
                for component, cb in ((0, cx), (1, cy)):
                    d = back * weighted(component, qr[lt][k], qc[lt][k]) + common
                    inv = 1.0 / (d + off - sbefore * cb)
                    c = scaled * inv
                    D[component * L + z, lt, rows(k), :] = d
                    I[component * L + z, lt, rows(k), :] = share * inv
                    C[component * L + z, lt, rows(k), :] = c
                    new.append(c)
                out += new
        return tuple(out)

    zero = jnp.zeros((8, 128), F32)
    lax.fori_loop(0, L, factor, (zero,) * 32, unroll=UNROLL)

    def forward(tiles):
        n = len(tiles)

        def step(z, carry):
            out = []
            for component in range(2):
                p = component * L + z
                y, yr, yc = around(X, p, tiles)
                for lt in range(2):
                    for i, k in enumerate(tiles):
                        t = FS[p, lt, rows(k), :] + weighted(component, yr[lt][i], yc[lt][i])
                        t = t + carry[(component * 2 + lt) * n + i]
                        T[p, lt, rows(k), :] = t
                        out.append(C[p, lt, rows(k), :] * t)
            return tuple(out)

        lax.fori_loop(0, L, step, (zero,) * (4 * n), unroll=UNROLL)

    def backward(tiles):
        n = len(tiles)

        def step(s, carry):
            z = L - 1 - s
            out = []
            for component in range(2):
                p = component * L + z
                for lt in range(2):
                    for i, k in enumerate(tiles):
                        new = I[p, lt, rows(k), :] * T[p, lt, rows(k), :] + C[p, lt, rows(k), :] * carry[(component * 2 + lt) * n + i]
                        X[p, lt, inside(k), :] = 0.2 * X[p, lt, inside(k), :] + new
                        out.append(new)
            return tuple(out)

        lax.fori_loop(0, L, step, (zero,) * (4 * n), unroll=UNROLL)

    def remainder(tiles, put):
        n = len(tiles)

        def step(z, carry):
            after = jnp.minimum(z + 1, L - 1)
            out = []
            for component in range(2):
                p = component * L + z
                y, yr, yc = around(X, p, tiles)
                got = []
                for lt in range(2):
                    for i, k in enumerate(tiles):
                        w = W[z, lt, rows(k), :]
                        r = FS[p, lt, rows(k), :] + weighted(component, yr[lt][i], yc[lt][i])
                        r = r - D[p, lt, rows(k), :] * y[lt][i]
                        r = r + w * X[after + component * L, lt, inside(k), :] + carry[(component * 2 + lt) * n + i]
                        got.append(Q[z, lt, inside(k), :] * r)
                        out.append(w * y[lt][i])
                put(component, z, got)
            return tuple(out)

        lax.fori_loop(0, L, step, (zero,) * (4 * n), unroll=UNROLL)

    pre = [0, 1, 2, 3]
    forward(pre)
    backward(pre)
    forward(pre)
    backward(pre)

    def put_rem(component, z, got):
        for lt in range(2):
            for i, k in enumerate(pre):
                T[component * L + z, lt, rows(k), :] = got[lt * 4 + i]

    remainder(pre, put_rem)

    even, odd = pl.ds(0, 16, stride=2), pl.ds(1, 16, stride=2)

    def gather(p, _):
        for lt in range(2):
            CA[lt, pl.ds(pl.multiple_of(p * 16, 16), 16), :] = T[p, lt, even, :] + T[p, lt, odd, :]
        return 0

    lax.fori_loop(0, 40, gather, 0, unroll=40)

    def gather_eta(z, _):
        for lt in range(2):
            CA[lt, pl.ds(pl.multiple_of((z + 40) * 16, 16), 16), :] = E[z, lt, even, :] + E[z, lt, odd, :]
        return 0

    lax.fori_loop(0, L, gather_eta, 0, unroll=UNROLL)
    for i in range(3):
        for lt in range(2):
            CA[lt, (60 + i) * 16 : (61 + i) * 16, :] = F[2 + i, lt, even, :] + F[2 + i, lt, odd, :]
    CB[...] = product(CA[0], restrict[0]) + product(CA[1], restrict[1])

    cmask = [jnp.where(CB[960 + 8 * k : 968 + 8 * k, :] > 0.0, 0.0, 1.0) for k in range(2)]
    cthick = [CB[976 + 8 * k : 984 + 8 * k, :] for k in range(2)]
    cih = [20.0 / jnp.where(t > 0.0, t, 1.0) for t in cthick]
    cdrag = [CB[992 + 8 * k : 1000 + 8 * k, :] * cih[k] for k in range(2)]

    def padded(p, k, by=0):
        return pl.ds(p * 16 + 8 * k + 8 + by, 8)

    def coarse_around(ref, p):
        here = [ref[padded(p, k), :] for k in range(2)]
        up_down = [(ref[padded(p, k, -1), :], ref[padded(p, k, 1), :]) for k in range(2)]
        return up_down, beside([here], lane)[0]

    for ref, size in ((CX, 40), (CQ, 20)):
        ref[0:8, :] = zero
        ref[16 * size + 8 : 16 * size + 16, :] = zero

    def at(p, k):
        return pl.ds(pl.multiple_of(p * 16 + 8 * k, 8), 8)

    def coarse_roots(z, _):
        for k in range(2):
            e = CB[at(40 + z, k), :]
            q = 0.5 * jnp.sqrt(e)
            back = jnp.where(e > 0.0, 1.0 / q, 0.0)
            CQ[padded(z, k), :] = q
            CR[at(z, k), :] = back
            for component in range(2):
                CB[at(component * L + z, k), :] = CB[at(component * L + z, k), :] * back
        return 0

    lax.fori_loop(0, L, coarse_roots, 0, unroll=UNROLL)

    def coarse_factor(z, carry):
        top = jnp.where(z < L - 1, 1.0, 0.0)
        bed = jnp.where(z == 0, 1.0, 0.0)
        after = jnp.minimum(z + 1, L - 1)
        qr, qc = coarse_around(CQ, z)
        out = []
        for k in range(2):
            wbefore, sbefore, cx, cy = carry[4 * k : 4 * k + 4]
            back = CR[at(z, k), :]
            w = (CB[at(40 + z, k), :] + CB[at(40 + after, k), :]) * (0.5 * top * (cih[k] * cih[k]))
            scaled = w * (back * CR[at(after, k), :])
            common = (w + wbefore + bed * cdrag[k]) * (back * back)
            new = [w, scaled]
            for component, cb in ((0, cx), (1, cy)):
                d = back * weighted(component, qr[k], qc[k]) + common
                inv = 1.0 / (d + cmask[k] - sbefore * cb)
                c = scaled * inv
                CI[at(component * L + z, k), :] = (0.8 - 0.8 * cmask[k]) * inv
                CC[at(component * L + z, k), :] = c
                new.append(c)
            out += new
        return tuple(out)

    lax.fori_loop(0, L, coarse_factor, (zero,) * 8, unroll=UNROLL)

    for turn in range(4):

        def coarse_forward(z, carry, turn=turn):
            out = []
            for component in range(2):
                p = component * L + z
                if turn > 0:
                    yr, yc = coarse_around(CX, p)
                for k in range(2):
                    t = CB[at(p, k), :] + carry[component * 2 + k]
                    if turn > 0:
                        t = t + weighted(component, yr[k], yc[k])
                    CT[at(p, k), :] = t
                    out.append(CC[at(p, k), :] * t)
            return tuple(out)

        lax.fori_loop(0, L, coarse_forward, (zero,) * 4, unroll=UNROLL)

        def coarse_backward(s, carry, turn=turn):
            z = L - 1 - s
            out = []
            for component in range(2):
                p = component * L + z
                for k in range(2):
                    new = CI[at(p, k), :] * CT[at(p, k), :] + CC[at(p, k), :] * carry[component * 2 + k]
                    if turn > 0:
                        CX[padded(p, k), :] = 0.2 * CX[padded(p, k), :] + new
                    else:
                        CX[padded(p, k), :] = new
                    out.append(new)
            return tuple(out)

        lax.fori_loop(0, L, coarse_backward, (zero,) * 4, unroll=UNROLL)

    def spread(p, _):
        CE[pl.ds(pl.multiple_of(p * 8, 8), 8), :] = pltpu.roll(
            jnp.where(low, CX[padded(p, 1), :] * CR[at(lax.rem(p, L), 1), :], CX[padded(p, 0), :] * CR[at(lax.rem(p, L), 0), :]), 4, 0
        )
        return 0

    lax.fori_loop(0, 40, spread, 0, unroll=40)
    for lt in range(2):
        CF[lt] = product(CE[...], expand[lt])

    def correct(p, _):
        for lt in range(2):
            tile = CF[lt, pl.ds(pl.multiple_of(p * 8, 8), 8), :]
            PC[p, lt, pl.ds(0, 8, stride=2), :] = tile
            PC[p, lt, pl.ds(1, 8, stride=2), :] = tile
            for k in (1, 2):
                q = Q[lax.rem(p, L), lt, inside(k), :]
                X[p, lt, inside(k), :] = X[p, lt, inside(k), :] + q * PC[p, lt, rows(k - 1), :]
        return 0

    lax.fori_loop(0, 40, correct, 0, unroll=40)

    post = [1, 2]
    for _ in range(2):
        forward(post)
        backward(post)

    def put_res(component, z, got):
        res_out[component, z] = pltpu.roll(jnp.where(low, got[1], got[0]), 4, 0)
        p = component * L + z
        vel = [X[p, 0, inside(k), :] * R[z, 0, rows(k), :] for k in (1, 2)]
        vel_out[component, z] = pltpu.roll(jnp.where(low, vel[1], vel[0]), 4, 0)

    remainder(post, put_res)


def transfer_matrices():
    lane = jnp.arange(128)
    main = lane // 2
    rim = jnp.where(lane < 16, 64 + lane // 2, jnp.where(lane >= 112, 120 + (lane - 112) // 2, -1))
    hits = jnp.stack([main, rim])[:, :, None] == lane[None, None, :]
    restrict = jnp.where(hits, 0.25, 0.0).astype(F32)
    expand = jnp.where(hits, 1.0, 0.0).astype(F32).transpose(0, 2, 1)
    twice = lambda w: jnp.concatenate([w, w], axis=1).astype(jnp.bfloat16)
    return twice(restrict), twice(expand)


def pairs(move):
    def of(axis):
        rows, cols = lax.axis_size("gx"), lax.axis_size("gy")
        count = rows if axis == "gx" else cols
        hops = [(i, move(i)) for i in range(count) if 0 <= move(i) < count]
        if axis == "gx":
            return [(i * cols + j, k * cols + j) for i, k in hops for j in range(cols)]
        return [(i * cols + j, i * cols + k) for i in range(rows) for j, k in hops]

    return of


def send(cells, axis, move):
    return lax.ppermute(cells, ("gx", "gy"), pairs(move)(axis))


def inner_swap(i):
    return i ^ 1


def outer_swap(i):
    return ((i + 1) ^ 1) - 1


def per_device(velocity, drive, stiffness, thickness, ice_mask, friction_class, friction_table):
    vmem = pl.BlockSpec(memory_space=pltpu.VMEM)
    smem = pl.BlockSpec(memory_space=pltpu.SMEM)
    main, strips = pl.pallas_call(
        pack_kernel,
        out_shape=(jax.ShapeDtypeStruct((PLANES, 8, 128), F32), jax.ShapeDtypeStruct((STRIPS, 8, 128), F32)),
        in_specs=[vmem] * 6 + [smem],
        out_specs=(vmem, vmem),
        name="pack",
    )(velocity, drive, stiffness, thickness, ice_mask, friction_class, friction_table)
    inner = send(strips, "gy", inner_swap)
    outer = send(strips, "gy", outer_swap)
    odd = lax.axis_index("gy") % 2 == 1
    left = jnp.where(odd, inner, outer)
    right = jnp.where(odd, outer, inner)
    lane = lax.broadcasted_iota(jnp.int32, strips.shape, 2)
    rim = jnp.where(lane % 32 < 16, left, right)
    whole = jnp.concatenate([main, rim], axis=0)
    before = send(whole, "gx", lambda i: i + 2)
    after = send(whole, "gx", lambda i: i - 2)
    inner = send(whole, "gx", inner_swap)
    outer = send(whole, "gx", outer_swap)
    parity = (lax.axis_index("gx") % 2).astype(jnp.int32).reshape(1)
    parts = (parity, before, outer, whole, inner, after)
    restrict, expand = transfer_matrices()
    fine = lambda n, r: pltpu.VMEM((n, 2, r, 128), F32)
    coarse = lambda n: pltpu.VMEM((16 * n, 128), F32)
    out = jax.ShapeDtypeStruct((2, L, 8, 128), F32)
    return pl.pallas_call(
        main_kernel,
        out_shape=(out, out),
        in_specs=[smem] + [vmem] * 7,
        out_specs=(vmem, vmem),
        scratch_shapes=[
            fine(40, 56), fine(5, 40), fine(20, 48), fine(20, 32), fine(20, 32), fine(20, 32), fine(40, 32), fine(40, 32),
            fine(40, 32), fine(40, 32), fine(40, 40), fine(40, 48),
            pltpu.VMEM((2, 63 * 16, 128), F32), coarse(63), pltpu.VMEM((320, 128), F32), pltpu.VMEM((2, 320, 128), F32),
            coarse(41), coarse(21), coarse(20), coarse(40), coarse(40), coarse(40), fine(40, 16),
        ],
        compiler_params=pltpu.CompilerParams(vmem_limit_bytes=48 * 1024 * 1024),
        name="cycle",
    )(*parts, restrict, expand)


def solution(mesh):
    return jax.shard_map(
        per_device,
        mesh=mesh,
        in_specs=(
            P(None, None, "gx", "gy"),
            P(None, "gx", "gy"),
            P("gx", "gy"),
            P("gx", "gy"),
            P("gx", "gy"),
            P("gx", "gy"),
            P(),
        ),
        out_specs=(P(None, None, "gx", "gy"), P(None, None, "gx", "gy")),
        check_vma=False,
    )
```
